128 devices in a mesh: replica: 4 (over y_lo, core), expert: 32 (over y_hi, z, x).
Axes of the slice: x: 4, y: 4 (y_hi: 2, y_lo: 2; y = y_hi * 2 + y_lo), z: 4, core: 2. Of those that a mesh axis runs over, the one named last changes fastest.
Arguments:
- hidden_in: bfloat16 [2048, 4096], P(('replica', 'expert')), may hold values from -6 to 6
- query: bfloat16 [2048, 8192], P(('replica', 'expert')), may hold values from -50 to 50
- key_new: bfloat16 [2048, 512], P(('replica', 'expert')), may hold values from -6 to 6
- value_new: bfloat16 [2048, 512], P(('replica', 'expert')), may hold values from -6 to 6
- key_cache: bfloat16 [2048, 4, 512, 128], P(('replica', 'expert')), may hold values from -6 to 6
- value_cache: bfloat16 [2048, 4, 512, 128], P(('replica', 'expert')), may hold values from -6 to 6
- cache_len: int32 [2048], P(('replica', 'expert')), may hold values from 2 to 512, as said below
- attn_out_w: bfloat16 [8192, 4096], P('expert', 'replica'), may hold values from -0.0625 to 0.0625
- norm_gain: float32 [4096], replicated, may hold values from 0.5 to 2
- routes: int32 [2048, 8], P(('replica', 'expert')), may hold values from 0 to 31, all different within a row; in each aligned block of 16 rows (0 to 15, 16 to 31, ...) at most 8 rows name the same one
- gate_weights: float32 [2048, 8], P(('replica', 'expert')), may hold values from 0.05 to 0.4
- w_gate: bfloat16 [32, 4096, 1536], P('expert', 'replica'), may hold values from -0.09375 to 0.09375
- w_up: bfloat16 [32, 4096, 1536], P('expert', 'replica'), may hold values from -0.09375 to 0.09375
- w_down: bfloat16 [32, 1536, 4096], P('expert', None, 'replica'), may hold values from -0.15625 to 0.15625
Outputs:
- layer_out: bfloat16 [2048, 4096], P(('replica', 'expert'))
The draws below stay inside these ranges and needn't reach their ends.
Inputs may be any that keep to these rules, and one draw needn't show every extreme that they name: `routes`: each row names 8 different experts; among the rows of one device no expert is named by more than 8 rows. `cache_len`: every row has at least two cached positions; some row has all 512.
All inputs are finite; a program needn't handle non-finite values.
Results may differ from the reference program's by a relative error of at most 0.015.
Values may be sent and summed in bfloat16 or wider, within the bound.
A program may use at most 192 MiB of HBM per device.

```python
import math
import jax
import jax.numpy as jnp
import numpy as np
from jax import lax

D = 4096
QH = 64
KVH = 4
HD = 128
HID = 1536
TOP = 8
EXPERTS = 32
ROWS_DEV = 16
CTX = 512
CAP = 8
BATCH = 2048
N_REPLICA = 4
N_EXPERT = 32


def draw_query(key, part):
    key = jax.random.fold_in(key, 1)
    values = jnp.clip(jax.random.normal(key, (BATCH, QH, HD), jnp.float32), -6.0, 6.0)
    return values.reshape(BATCH, QH * HD).astype(jnp.bfloat16)


def draw_key_cache(key, part):
    key = jax.random.fold_in(key, 2)
    values = jnp.clip(jax.random.normal(key, (BATCH, KVH, CTX, HD), jnp.float32), -6.0, 6.0)
    return values.astype(jnp.bfloat16)


def draw_cache_len(key, part):
    key = jax.random.fold_in(key, 3)
    lengths = jax.random.randint(key, (BATCH,), 2, CTX + 1)
    spot = jax.random.randint(jax.random.fold_in(key, 7), (), 0, BATCH)
    return lengths.at[spot].set(CTX).astype(jnp.int32)


def block_scale(rng, dims, cuts, smallest, largest):
    level, own = 1.0, jax.random.fold_in(rng, 6)
    for dim, parts in cuts:
        steps = jnp.exp(jax.random.uniform(jax.random.fold_in(own, dim), (parts,), jnp.float32, smallest / len(cuts), largest / len(cuts)))
        level = level * jnp.repeat(steps, dims[dim] // parts).reshape([-1 if axis == dim else 1 for axis in range(len(dims))])
    return level


def deal_out(key, own, number, rows, number_of, top, reach, lean):
    ranking = jax.random.permutation(key, number_of)
    heavy_load, common = load_shares(number_of, rows * top, reach, lean, True), load_shares(number_of, rows * top, reach, lean, False)
    places = jnp.arange(number_of)

    def named(tallies, offset_by):
        used = int((tallies > 0).sum())
        fixed = max(1, used // 4)
        shifted = fixed + (places - fixed + offset_by * (used - fixed)) % max(1, number_of - fixed)
        return jnp.zeros((number_of,), jnp.int32).at[ranking[jnp.where(places < fixed, places, shifted)]].set(jnp.asarray(tallies, jnp.int32))

    tallies = jnp.where(number % 4 == 0, named(heavy_load, number // 4), named(common, number - number // 4 - 1))
    mixed = jax.random.permutation(jax.random.fold_in(own, 3), number_of)
    source_of, taker = mixed[0:number_of // 2 * 2:2], mixed[1:number_of // 2 * 2:2]
    slack = jnp.minimum(tallies[source_of] - 1, reach - tallies[taker]) // 2
    slack = jnp.where((source_of == ranking[0]) | (taker == ranking[0]) | (tallies[taker] == 0), 0, jnp.maximum(slack, 0))
    shifted = jax.random.randint(jax.random.fold_in(own, 4), (number_of // 2,), 0, 1 << 20) % (slack + 1)
    tallies = tallies.at[source_of].add(-shifted).at[taker].add(shifted)
    items = jnp.searchsorted(jnp.cumsum(tallies), jnp.arange(rows * top), side="right").astype(jnp.int32)
    listing = items.reshape(top, rows).T
    listing = listing[jax.random.permutation(jax.random.fold_in(own, 1), rows)]
    offset_by = jax.random.randint(jax.random.fold_in(own, 2), (rows, 1), 0, top)
    return jnp.take_along_axis(listing, (jnp.arange(top)[None, :] + offset_by) % top, axis=1)


def load_shares(amount, total, limit, lean, full):
    portions = [(1 << 20) // math.isqrt(standing ** lean) + 1 for standing in range(1, amount + 1)]
    largest = limit if full else min(limit, max(-(-total // amount), total * portions[0] // sum(portions)))
    least = 1 if total - largest >= amount - 1 else 0
    given, surplus = [largest] + [least] * (amount - 1), total - largest - least * (amount - 1)
    while surplus > 0:
        free = [i for i in range(1, amount) if given[i] < largest] or [i for i in range(1, amount) if given[i] < limit]
        whole, budget = sum([portions[i] for i in free]), surplus
        for i in free:
            addition = min(limit - given[i], max(1, budget * portions[i] // whole), surplus)
            given[i] = given[i] + addition
            surplus = surplus - addition
    return np.array(given)


def centred(key, extent, spread, limit, split=(), held_as=jnp.bfloat16):
    gain = block_scale(key, extent, split, -0.22, 0.18) if split else 1.0
    values = jax.random.normal(key, extent, jnp.float32) * spread * gain
    return jnp.minimum(jnp.maximum(values, -limit), limit).astype(held_as)


def setup_inputs(seed: int = 0) -> dict:
    arg_keys = jax.random.split(jax.random.key(seed), 15)
    hidden_in = centred(arg_keys[0], (BATCH, D), 1.0, 6.0, ((0, 128),))
    query = draw_query(jax.random.fold_in(arg_keys[14], 71), 0)
    key_new = centred(arg_keys[2], (BATCH, KVH * HD), 1.0, 6.0, ((0, 128),))
    value_new = centred(arg_keys[3], (BATCH, KVH * HD), 1.0, 6.0, ((0, 128),))
    key_cache = draw_key_cache(jax.random.fold_in(arg_keys[14], 71), 0)
    value_cache = centred(arg_keys[5], (BATCH, KVH, CTX, HD), 1.0, 6.0, ((0, 128),))
    cache_len = draw_cache_len(jax.random.fold_in(arg_keys[14], 71), 0)
    attn_out_w = centred(arg_keys[7], (QH * HD, D), (QH * HD) ** -0.5, 0.0625, ((0, 32), (1, 4)))
    norm_gain = jnp.clip(jnp.exp(jax.random.uniform(arg_keys[8], (D,), jnp.float32, math.log(0.5), math.log(2.0))), 0.5, 2.0)
    routes_keys = jax.random.split(jax.random.fold_in(arg_keys[9], 1), BATCH // ROWS_DEV)
    routes_turns = jax.random.permutation(jax.random.fold_in(arg_keys[9], 3), BATCH // ROWS_DEV)
    routes = jax.vmap(lambda own, number: deal_out(jax.random.fold_in(arg_keys[9], 2), own, number, ROWS_DEV, EXPERTS, TOP, CAP, 1))(routes_keys, routes_turns).reshape((BATCH, TOP))
    gate_weights = jnp.clip(jnp.exp(math.log(0.4) - 2.0794415 * jax.random.uniform(arg_keys[10], (BATCH, TOP), jnp.float32) ** block_scale(arg_keys[10], (BATCH, TOP), ((0, 128),), -0.2, 0.2)), 0.05, 0.4)
    w_gate = centred(arg_keys[11], (EXPERTS, D, HID), D ** -0.5, 0.09375, ((0, 32), (1, 4)))
    w_up = centred(arg_keys[12], (EXPERTS, D, HID), D ** -0.5, 0.09375, ((0, 32), (1, 4)))
    w_down = centred(arg_keys[13], (EXPERTS, HID, D), HID ** -0.5, 0.15625, ((0, 32), (2, 4)))
    return dict(hidden_in=hidden_in, query=query, key_new=key_new, value_new=value_new, key_cache=key_cache, value_cache=value_cache, cache_len=cache_len, attn_out_w=attn_out_w, norm_gain=norm_gain, routes=routes, gate_weights=gate_weights, w_gate=w_gate, w_up=w_up, w_down=w_down)


def attend_block(query, key_new, value_new, key_cache, value_cache, cache_len):
    rows = query.shape[0]
    grouped = QH // KVH
    scale = HD ** (-0.5)
    queries = query.reshape(rows, KVH, grouped, HD).astype(jnp.float32)
    cached = jnp.einsum('rgqd,rgpd->rgqp', queries, key_cache.astype(jnp.float32)) * scale
    own = jnp.einsum('rgqd,rgd->rgq', queries, key_new.reshape(rows, KVH, HD).astype(jnp.float32)) * scale
    live = jnp.arange(CTX)[None, :] < cache_len[:, None]
    cached = jnp.where(live[:, None, None, :], cached, -jnp.inf)
    highest = jnp.maximum(lax.optimization_barrier(jnp.max(cached, axis=-1)), own)
    cached_exp = jnp.exp(cached - highest[..., None])
    own_exp = jnp.exp(own - highest)
    total = lax.optimization_barrier(jnp.sum(cached_exp, axis=-1)) + own_exp
    cached_prob = (cached_exp / total[..., None]).astype(jnp.bfloat16)
    own_prob = (own_exp / total).astype(jnp.bfloat16)
    mixed = jnp.einsum('rgqp,rgpd->rgqd', cached_prob.astype(jnp.float32), value_cache.astype(jnp.float32))
    mixed = mixed + own_prob.astype(jnp.float32)[..., None] * value_new.reshape(rows, KVH, 1, HD).astype(jnp.float32)
    return mixed.reshape(rows, QH * HD).astype(jnp.bfloat16)

def reference(hidden_in, query, key_new, value_new, key_cache, value_cache, cache_len, attn_out_w, norm_gain, routes, gate_weights, w_gate, w_up, w_down):
    devices = N_REPLICA * N_EXPERT
    rows_all = hidden_in.shape[0]

    def blocked(array):
        return array.reshape((devices, ROWS_DEV) + array.shape[1:])

    def attend_one(pieces):
        return attend_block(*pieces)
    attn = lax.map(attend_one, (blocked(query), blocked(key_new), blocked(value_new), blocked(key_cache), blocked(value_cache), blocked(cache_len)))
    attn = attn.reshape(rows_all, QH * HD)
    mid = hidden_in.astype(jnp.float32) + jnp.dot(attn, attn_out_w, preferred_element_type=jnp.float32)
    normed = (mid * lax.rsqrt(lax.optimization_barrier(jnp.mean(mid * mid, axis=-1, keepdims=True)) + 1e-06) * norm_gain).astype(jnp.bfloat16)
    flat = routes.reshape(devices, ROWS_DEV * TOP)
    onehot = (flat[..., None] == jnp.arange(EXPERTS)[None, None, :]).astype(jnp.int32)
    rank = lax.optimization_barrier(jnp.sum((jnp.cumsum(onehot, axis=1) - 1) * onehot, axis=2))
    place = (jnp.arange(devices)[:, None] * CAP + rank).reshape(-1).astype(jnp.int32)
    expert_of = flat.reshape(-1).astype(jnp.int32)
    row_of = jnp.repeat(jnp.arange(rows_all), TOP).astype(jnp.int32)
    table = jnp.full((EXPERTS, devices * CAP), rows_all, jnp.int32).at[expert_of, place].set(row_of)
    padded = jnp.concatenate([normed, jnp.zeros((1, D), jnp.bfloat16)], axis=0)

    def run_expert(pieces):
        index, gate_mat, up_mat, down_mat = pieces
        inputs = padded[index]
        gate = jnp.dot(inputs, gate_mat, preferred_element_type=jnp.float32)
        up_val = jnp.dot(inputs, up_mat, preferred_element_type=jnp.float32)
        units = (jax.nn.silu(gate) * up_val).astype(jnp.bfloat16)
        return jnp.dot(units, down_mat, preferred_element_type=jnp.float32).astype(jnp.bfloat16)
    results = lax.map(run_expert, (table, w_gate, w_up, w_down))
    picked = results[expert_of, place].reshape(rows_all, TOP, D)
    mixture = lax.optimization_barrier(jnp.sum(gate_weights[..., None] * picked.astype(jnp.float32), axis=1))
    return (mid + mixture).astype(jnp.bfloat16)
```

```python
import jax
import jax.numpy as jnp
from jax import lax
from jax.sharding import PartitionSpec as P

HD = 128
TOP = 8
EXPERTS = 32
CAP = 8
LINE = 4
GROUPS = 8
SWAP_Y = [(0, 2), (1, 3), (2, 0), (3, 1)]
SWAP_CORE = [(0, 1), (1, 0), (2, 3), (3, 2)]
SAME_X = [[x + LINE * a for a in range(GROUPS)] for x in range(LINE)]


def attend_local(query, key_new, value_new, key_cache, value_cache, cache_len):
    rows = query.shape[0]
    kv_heads = key_cache.shape[1]
    context = key_cache.shape[2]
    head_size = key_cache.shape[3]
    grouped = query.shape[1] // (kv_heads * head_size)
    scale = HD ** (-0.5)
    queries = query.reshape(rows, kv_heads, grouped, head_size)
    cached = (
        jnp.einsum("rgqd,rgpd->rgqp", queries, key_cache, preferred_element_type=jnp.float32)
        * scale
    )
    own = (
        jnp.einsum(
            "rgqd,rgd->rgq",
            queries,
            key_new.reshape(rows, kv_heads, head_size),
            preferred_element_type=jnp.float32,
        )
        * scale
    )
    live = jnp.arange(context)[None, :] < cache_len[:, None]
    cached = jnp.where(live[:, None, None, :], cached, -jnp.inf)
    highest = jnp.maximum(jnp.max(cached, axis=-1), own)
    cached_exp = jnp.exp(cached - highest[..., None])
    own_exp = jnp.exp(own - highest)
    total = jnp.sum(cached_exp, axis=-1) + own_exp
    cached_prob = (cached_exp / total[..., None]).astype(jnp.bfloat16)
    own_prob = (own_exp / total).astype(jnp.bfloat16)
    mixed = jnp.einsum(
        "rgqp,rgpd->rgqd", cached_prob, value_cache, preferred_element_type=jnp.float32
    )
    mixed = mixed + own_prob.astype(jnp.float32)[..., None] * value_new.reshape(
        rows, kv_heads, 1, head_size
    ).astype(jnp.float32)
    return mixed.reshape(rows, grouped * kv_heads * head_size).astype(jnp.bfloat16)


def swap_y(value):
    return lax.ppermute(value, "replica", SWAP_Y)


def swap_core(value):
    return lax.ppermute(value, "replica", SWAP_CORE)


def same_x(value):
    return lax.all_to_all(
        value, "expert", split_axis=0, concat_axis=0, axis_index_groups=SAME_X, tiled=True
    )


def from_x(value, step):
    pairs = [
        (e, e // LINE * LINE + (e + LINE - step) % LINE) for e in range(EXPERTS)
    ]
    return lax.ppermute(value, "expert", pairs)


def relative(quarters, replica):
    core, chip = replica % 2, replica // 2
    a, b, c, d = quarters
    a, b, c, d = (
        jnp.where(core == 0, a, b),
        jnp.where(core == 0, b, a),
        jnp.where(core == 0, c, d),
        jnp.where(core == 0, d, c),
    )
    return (
        jnp.where(chip == 0, a, c),
        jnp.where(chip == 0, b, d),
        jnp.where(chip == 0, c, a),
        jnp.where(chip == 0, d, b),
    )


def body(
    hidden_in,
    query,
    key_new,
    value_new,
    key_cache,
    value_cache,
    cache_len,
    attn_out_w,
    norm_gain,
    routes,
    gate_weights,
    w_gate,
    w_up,
    w_down,
):
    f32, bf16 = jnp.float32, jnp.bfloat16
    rows = hidden_in.shape[0]
    width = hidden_in.shape[1]
    quarter = width // 4
    replica = lax.axis_index("replica")
    x = lax.axis_index("expert") % LINE

    proj = jnp.concatenate([attn_out_w] + [from_x(attn_out_w, s) for s in range(1, LINE)], axis=0)
    proj = jnp.concatenate([proj, swap_core(proj)], axis=1)
    gate_mats = (w_gate[0], swap_core(w_gate)[0])
    up_mats = (w_up[0], swap_core(w_up)[0])
    down_mats = (w_down[0], swap_core(w_down)[0])

    hid = relative([hidden_in[:, q * quarter : (q + 1) * quarter] for q in range(4)], replica)
    hid_here = jnp.concatenate(hid[:2], axis=1)
    hid_there = swap_y(jnp.concatenate(hid[2:], axis=1))
    hid = jnp.concatenate([hid_here, hid_there], axis=0).astype(f32)
    gain = relative([norm_gain[q * quarter : (q + 1) * quarter] for q in range(4)], replica)
    gain = jnp.concatenate(gain[:2])

    route2 = jnp.stack([routes, swap_y(routes)])
    weight2 = jnp.stack([gate_weights, swap_y(gate_weights)])
    flat = route2.reshape(2, rows * TOP)
    onehot = (flat[:, :, None] == jnp.arange(EXPERTS)[None, None, :]).astype(jnp.int32)
    rank = jnp.sum((jnp.cumsum(onehot, axis=1) - 1) * onehot, axis=2)
    target = (flat * CAP + rank).reshape(2, rows, TOP)
    chosen = target[..., None] == jnp.arange(EXPERTS * CAP)
    placing = jnp.any(chosen, axis=2).astype(bf16)
    weighting = jnp.sum(jnp.where(chosen, weight2[..., None], 0.0), axis=2)

    attn = attend_local(query, key_new, value_new, key_cache, value_cache, cache_len)
    heads = attn.reshape(rows, GROUPS, LINE, -1)
    heads = lax.dynamic_slice_in_dim(jnp.concatenate([heads, heads], axis=2), x, LINE, axis=2)
    heads = heads.reshape(rows, GROUPS, -1).transpose(1, 0, 2)
    heads = same_x(heads)
    heads = jnp.stack([heads, swap_y(heads)], axis=1)
    part = jnp.dot(heads.reshape(GROUPS * 2 * rows, -1), proj, preferred_element_type=f32)
    part = same_x(part.astype(bf16).reshape(GROUPS, 2 * rows, 2 * quarter))
    mid = hid + jnp.sum(part.astype(f32), axis=0)

    squares = jnp.sum(mid * mid, axis=-1)
    there = swap_y(squares)
    squares = squares + jnp.concatenate([there[rows:], there[:rows]])
    normed = (mid * lax.rsqrt(squares / width + 1e-06)[:, None] * gain).astype(bf16)

    outgoing = jnp.einsum(
        "hrs,hrd->hsd", placing, normed.reshape(2, rows, 2 * quarter), preferred_element_type=f32
    ).astype(bf16)
    outgoing = outgoing.reshape(2, EXPERTS, CAP, 2 * quarter).transpose(1, 0, 2, 3)
    block = lax.all_to_all(outgoing, "expert", split_axis=0, concat_axis=0, tiled=True)
    block = block.transpose(1, 0, 2, 3).reshape(2 * EXPERTS * CAP, 2 * quarter)
    ours, theirs = block[:, :quarter], block[:, quarter:]

    def partial(mats):
        return jnp.dot(ours, mats[0], preferred_element_type=f32) + jnp.dot(
            theirs, mats[1], preferred_element_type=f32
        )

    half = EXPERTS * CAP
    gate, up_val = partial(gate_mats), partial(up_mats)
    gate = gate[:half] + swap_y(gate[half:].astype(bf16)).astype(f32)
    up_val = up_val[:half] + swap_y(up_val[half:].astype(bf16)).astype(f32)
    units = (jax.nn.silu(gate) * up_val).astype(bf16)
    units = jnp.concatenate([units, swap_y(units)], axis=0)
    result = jnp.concatenate(
        [jnp.dot(units, mat, preferred_element_type=f32).astype(bf16) for mat in down_mats], axis=1
    )
    result = result.reshape(2, EXPERTS, CAP, 2 * quarter).transpose(1, 0, 2, 3)
    returned = lax.all_to_all(result, "expert", split_axis=0, concat_axis=0, tiled=True)
    returned = returned.transpose(1, 0, 2, 3).reshape(2, EXPERTS * CAP, 2 * quarter)
    mixture = jnp.einsum(
        "hrs,hsd->hrd", weighting, returned.astype(f32), precision=lax.Precision.HIGHEST
    )
    out = (mid + mixture.reshape(2 * rows, 2 * quarter)).astype(bf16)
    there = swap_y(out[rows:])
    here = out[:rows]
    return jnp.concatenate(
        relative(
            (here[:, :quarter], here[:, quarter:], there[:, :quarter], there[:, quarter:]), replica
        ),
        axis=1,
    )


def solution(mesh):
    placed = (
        P(("replica", "expert"), None),
        P(("replica", "expert"), None),
        P(("replica", "expert"), None),
        P(("replica", "expert"), None),
        P(("replica", "expert"), None, None, None),
        P(("replica", "expert"), None, None, None),
        P(("replica", "expert")),
        P("expert", "replica"),
        P(),
        P(("replica", "expert"), None),
        P(("replica", "expert"), None),
        P("expert", "replica", None),
        P("expert", "replica", None),
        P("expert", None, "replica"),
    )
    return jax.shard_map(
        body, mesh=mesh, in_specs=placed, out_specs=P(("replica", "expert"), None), check_vma=False
    )
```

```python
import jax
import jax.numpy as jnp
from jax import lax
from jax.experimental import pallas as pl
from jax.experimental.pallas import tpu as pltpu
from jax.sharding import PartitionSpec as P

MESH = pl.DeviceIdType.MESH

HD = 128
TOP = 8
EXPERTS = 32
CAP = 8
LINE = 4
GROUPS = 8
SWAP_Y = [(0, 2), (1, 3), (2, 0), (3, 1)]
SWAP_CORE = [(0, 1), (1, 0), (2, 3), (3, 2)]
SAME_X = [[x + LINE * a for a in range(GROUPS)] for x in range(LINE)]


def attend_local(query, key_new, value_new, key_cache, value_cache, cache_len):
    rows = query.shape[0]
    kv_heads = key_cache.shape[1]
    context = key_cache.shape[2]
    head_size = key_cache.shape[3]
    grouped = query.shape[1] // (kv_heads * head_size)
    scale = HD ** (-0.5)
    queries = query.reshape(rows, kv_heads, grouped, head_size)
    cached = (
        jnp.einsum("rgqd,rgpd->rgqp", queries, key_cache, preferred_element_type=jnp.float32)
        * scale
    )
    own = (
        jnp.einsum(
            "rgqd,rgd->rgq",
            queries,
            key_new.reshape(rows, kv_heads, head_size),
            preferred_element_type=jnp.float32,
        )
        * scale
    )
    live = jnp.arange(context)[None, :] < cache_len[:, None]
    cached = jnp.where(live[:, None, None, :], cached, -jnp.inf)
    highest = jnp.maximum(jnp.max(cached, axis=-1), own)
    cached_exp = jnp.exp(cached - highest[..., None])
    own_exp = jnp.exp(own - highest)
    total = jnp.sum(cached_exp, axis=-1) + own_exp
    cached_prob = (cached_exp / total[..., None]).astype(jnp.bfloat16)
    own_prob = (own_exp / total).astype(jnp.bfloat16)
    mixed = jnp.einsum(
        "rgqp,rgpd->rgqd", cached_prob, value_cache, preferred_element_type=jnp.float32
    )
    mixed = mixed + own_prob.astype(jnp.float32)[..., None] * value_new.reshape(
        rows, kv_heads, 1, head_size
    ).astype(jnp.float32)
    return mixed.reshape(rows, grouped * kv_heads * head_size).astype(jnp.bfloat16)


def swap_y(value):
    return lax.ppermute(value, "replica", SWAP_Y)


def swap_core(value):
    return lax.ppermute(value, "replica", SWAP_CORE)


def swap_plane(value):
    return lax.ppermute(value, "expert", [(e, (e + 16) % EXPERTS) for e in range(EXPERTS)])


def same_x(value):
    return lax.all_to_all(
        value, "expert", split_axis=0, concat_axis=0, axis_index_groups=SAME_X, tiled=True
    )


def from_x(value, step):
    pairs = [
        (e, e // LINE * LINE + (e + LINE - step) % LINE) for e in range(EXPERTS)
    ]
    return lax.ppermute(value, "expert", pairs)


def relative(quarters, replica):
    core, chip = replica % 2, replica // 2
    a, b, c, d = quarters
    a, b, c, d = (
        jnp.where(core == 0, a, b),
        jnp.where(core == 0, b, a),
        jnp.where(core == 0, c, d),
        jnp.where(core == 0, d, c),
    )
    return (
        jnp.where(chip == 0, a, c),
        jnp.where(chip == 0, b, d),
        jnp.where(chip == 0, c, a),
        jnp.where(chip == 0, d, b),
    )


def offset(s):
    dz = s % 8 // 2
    return dz, 2 * (s % 2) + (dz + s // 8) % 2


def shifted(expert, s, sign):
    dz, dx = offset(s)
    plane, z, x = expert // 16, expert // 4 % 4, expert % 4
    return plane * 16 + (z + 4 + sign * dz) % 4 * 4 + (x + 4 + sign * dx) % 4


def moe_kernel(
    mid_ref,
    gain_ref,
    placing_ref,
    weighting_ref,
    wg0,
    wg1,
    wu0,
    wu1,
    wd0,
    wd1,
    out_ref,
    v_gate,
    v_up,
    v_down,
    square_out,
    square_in,
    scaled,
    scaled_in,
    rows_all,
    outgoing,
    block,
    part_out,
    part_in,
    part_own,
    units,
    result,
    returned,
    mixed,
    last_out,
    last_bf,
    last_in,
    last_bf_in,
    w_sem,
    pre_send,
    pre_recv,
    disp_send,
    disp_recv,
    part_send,
    part_recv,
    unit_send,
    unit_recv,
    ret_send,
    ret_recv,
    last_send,
    last_recv,
):
    f32, bf16 = jnp.float32, jnp.bfloat16
    replica, expert = lax.axis_index("replica"), lax.axis_index("expert")
    other_replica, other_plane = (replica + 2) % 4, (expert + 16) % 32
    beside = (other_replica, expert)
    across = (replica, other_plane)
    diagonal = (other_replica, other_plane)
    tile = 512
    hidden = v_gate.shape[2]
    quarter = v_gate.shape[1]
    half = 2 * quarter

    loads = [
        pltpu.make_async_copy(src, dst, w_sem.at[i])
        for i, (src, dst) in enumerate(
            [
                (wg0, v_gate.at[0]),
                (wg1, v_gate.at[1]),
                (wu0, v_up.at[0]),
                (wu1, v_up.at[1]),
                (wd0, v_down.at[0]),
                (wd1, v_down.at[1]),
            ]
        )
    ]
    for load in loads:
        load.start()

    barrier = pltpu.get_barrier_semaphore()

    @pl.loop(1, 16)
    def _(s):
        pl.semaphore_signal(
            barrier, inc=1, device_id=(replica, shifted(expert, s, 1)), device_id_type=MESH
        )

    for device in (beside, across, diagonal):
        pl.semaphore_signal(barrier, inc=1, device_id=device, device_id_type=MESH)
    pl.semaphore_wait(barrier, 18)

    def remote(src, dst, send, recv, device):
        return pltpu.make_async_remote_copy(
            src_ref=src,
            dst_ref=dst,
            send_sem=send,
            recv_sem=recv,
            device_id=device,
            device_id_type=MESH,
        )

    mid = mid_ref[...]
    square_out[...] = jnp.broadcast_to(jnp.sum(mid * mid, axis=-1, keepdims=True), (32, 128))
    scaled[...] = (mid * gain_ref[...]).astype(bf16)
    pre = [
        remote(square_out, square_in.at[i], pre_send.at[i], pre_recv.at[i], device)
        for i, device in enumerate((beside, across, diagonal))
    ]
    pre.append(remote(scaled, scaled_in, pre_send.at[3], pre_recv.at[3], across))
    for copy in (pre[3], pre[0], pre[1], pre[2]):
        copy.start()
    for copy in pre:
        copy.wait_recv()
    for h in range(2):
        here, there = pl.ds(16 * h, 16), pl.ds(16 * (1 - h), 16)
        width = 2.0 * half
        total = square_out[here, :1] + square_in[0, there, :1]
        normed = mid_ref[here, :] * gain_ref[...] * lax.rsqrt(total / width + 1e-06)
        rows_all[h, :16, :] = normed.astype(bf16)
        total = square_in[1, here, :1] + square_in[2, there, :1]
        normed = scaled_in[here, :].astype(f32) * lax.rsqrt(total / width + 1e-06)
        rows_all[h, 16:, :] = normed.astype(bf16)

    def dispatch(h, s):
        rows = pl.ds(pl.multiple_of(s * 16, 16), 16)
        return remote(
            outgoing.at[h, rows],
            block.at[h, rows],
            disp_send.at[h, s],
            disp_recv.at[h, s],
            (replica, shifted(expert, s, 1)),
        )

    for h in (1, 0):

        @pl.loop(0, half // tile)
        def _(n):
            cols = pl.ds(pl.multiple_of(n * tile, tile), tile)
            outgoing[h, :, cols] = jnp.dot(
                placing_ref[h], rows_all[h, :, cols], preferred_element_type=f32
            ).astype(bf16)

        @pl.loop(1, 16)
        def _(s):
            dispatch(h, s).start()

        block[h, :16, :] = outgoing[h, :16, :]

    def gate_up(h, start, count, store):
        rows = pl.ds(start, count)

        @pl.loop(0, hidden // tile)
        def _(n):
            at = pl.multiple_of(n * tile, tile)
            for which, mats in enumerate((v_gate, v_up)):
                value = jnp.dot(
                    block[h, rows, :quarter],
                    mats[0, :, pl.ds(at, tile)],
                    preferred_element_type=f32,
                ) + jnp.dot(
                    block[h, rows, quarter:],
                    mats[1, :, pl.ds(at, tile)],
                    preferred_element_type=f32,
                )
                store(which, pl.ds(at, tile), value)

    parts = [
        remote(part_out.at[c], part_in.at[c], part_send.at[c], part_recv.at[c], beside)
        for c in range(2)
    ]
    for load in loads[:4]:
        load.wait()
    for c in range(2):

        @pl.loop(max(1, 8 * c), 8 * c + 8)
        def _(s):
            dispatch(1, s).wait_recv()

        def store_out(which, cols, value):
            part_out[c, which, :, cols] = value.astype(bf16)

        gate_up(1, 128 * c, 128, store_out)
        parts[c].start()

    @pl.loop(1, 16)
    def _(s):
        dispatch(0, s).wait_recv()

    def store_own(which, cols, value):
        part_own[which, :, cols] = value

    gate_up(0, 0, 256, store_own)

    def give_back(h, s):
        rows = pl.ds(pl.multiple_of(s * 16, 16), 16)
        return remote(
            result.at[h, rows],
            returned.at[h, rows],
            ret_send.at[h, s],
            ret_recv.at[h, s],
            (replica, shifted(expert, s, -1)),
        )

    def down(h, c):
        for q in range(2):

            @pl.loop(0, quarter // tile)
            def _(n):
                at = pl.multiple_of(n * tile, tile)
                result[h, pl.ds(128 * c, 128), pl.ds(q * quarter + at, tile)] = jnp.dot(
                    units[h, c], v_down[q, :, pl.ds(at, tile)], preferred_element_type=f32
                ).astype(bf16)

        @pl.loop(max(1, 8 * c), 8 * c + 8)
        def _(s):
            give_back(h, s).start()

        if c == 0:
            returned[h, :16, :] = result[h, :16, :]

    sends = [
        remote(units.at[0, c], units.at[1, c], unit_send.at[c], unit_recv.at[c], beside)
        for c in range(2)
    ]
    for c in range(2):
        parts[c].wait_recv()

        @pl.loop(0, hidden // tile)
        def _(n):
            cols = pl.ds(pl.multiple_of(n * tile, tile), tile)
            rows = pl.ds(128 * c, 128)
            gate = part_own[0, rows, cols] + part_in[c, 0, :, cols].astype(f32)
            up_val = part_own[1, rows, cols] + part_in[c, 1, :, cols].astype(f32)
            units[0, c, :, cols] = (gate / (1.0 + jnp.exp(-gate)) * up_val).astype(bf16)

        sends[c].start()
        if c == 0:
            loads[4].wait()
            loads[5].wait()
        down(0, c)
    for c in range(2):
        sends[c].wait_recv()
        down(1, c)

    for h in range(2):

        @pl.loop(1, 16)
        def _(s):
            give_back(h, s).wait_recv()

    @pl.loop(0, half // tile)
    def _(n):
        cols = pl.ds(pl.multiple_of(n * tile, tile), tile)
        for h in range(2):
            three = jnp.dot(weighting_ref[h], returned[h, :, cols], preferred_element_type=f32)
            mixed[h, :, cols] = three[:32] + three[32:64] + three[64:]

    last_out[...] = mid_ref[16:, :] + mixed[1, :16, :]
    last_bf[0] = mixed[0, 16:, :].astype(bf16)
    last_bf[1] = mixed[1, 16:, :].astype(bf16)
    last = [
        remote(last_out, last_in, last_send.at[0], last_recv.at[0], beside),
        remote(last_bf.at[0], last_bf_in.at[0], last_send.at[1], last_recv.at[1], across),
        remote(last_bf.at[1], last_bf_in.at[1], last_send.at[2], last_recv.at[2], diagonal),
    ]
    for copy in last:
        copy.start()
    for copy in last:
        copy.wait_recv()
    out_ref[0] = (mid_ref[:16, :] + mixed[0, :16, :] + last_bf_in[0].astype(f32)).astype(bf16)
    out_ref[1] = (last_in[...] + last_bf_in[1].astype(f32)).astype(bf16)

    for copy in pre + parts + sends + last:
        copy.wait_send()
    for h in range(2):

        @pl.loop(1, 16)
        def _(s):
            dispatch(h, s).wait_send()
            give_back(h, s).wait_send()


def moe(mid, gain, placing, weighting, gate_mats, up_mats, down_mats):
    f32, bf16 = jnp.float32, jnp.bfloat16
    quarter, hidden = gate_mats[0].shape
    half = 2 * quarter
    vmem, anywhere = pl.BlockSpec(memory_space=pltpu.VMEM), pl.BlockSpec(memory_space=pl.ANY)
    dma = pltpu.SemaphoreType.DMA
    return pl.pallas_call(
        moe_kernel,
        out_shape=jax.ShapeDtypeStruct((2, 16, half), bf16),
        in_specs=[vmem] * 4 + [anywhere] * 6,
        out_specs=vmem,
        scratch_shapes=[
            pltpu.VMEM((2, quarter, hidden), bf16),
            pltpu.VMEM((2, quarter, hidden), bf16),
            pltpu.VMEM((2, hidden, quarter), bf16),
            pltpu.VMEM((32, 128), f32),
            pltpu.VMEM((3, 32, 128), f32),
            pltpu.VMEM((32, half), bf16),
            pltpu.VMEM((32, half), bf16),
            pltpu.VMEM((2, 32, half), bf16),
            pltpu.VMEM((2, 256, half), bf16),
            pltpu.VMEM((2, 256, half), bf16),
            pltpu.VMEM((2, 2, 128, hidden), bf16),
            pltpu.VMEM((2, 2, 128, hidden), bf16),
            pltpu.VMEM((2, 256, hidden), f32),
            pltpu.VMEM((2, 2, 128, hidden), bf16),
            pltpu.VMEM((2, 256, half), bf16),
            pltpu.VMEM((2, 256, half), bf16),
            pltpu.VMEM((2, 32, half), f32),
            pltpu.VMEM((16, half), f32),
            pltpu.VMEM((2, 16, half), bf16),
            pltpu.VMEM((16, half), f32),
            pltpu.VMEM((2, 16, half), bf16),
            dma((6,)),
            dma((4,)),
            dma((4,)),
            dma((2, 16)),
            dma((2, 16)),
            dma((2,)),
            dma((2,)),
            dma((2,)),
            dma((2,)),
            dma((2, 16)),
            dma((2, 16)),
            dma((3,)),
            dma((3,)),
        ],
        compiler_params=pltpu.CompilerParams(
            collective_id=0, has_side_effects=True, vmem_limit_bytes=50 * 1024 * 1024
        ),
        cost_estimate=pl.CostEstimate(
            flops=10 * 10**9, bytes_accessed=20 * 10**6, transcendentals=10**6
        ),
    )(mid, gain, placing, weighting, *gate_mats, *up_mats, *down_mats)


def body(
    hidden_in,
    query,
    key_new,
    value_new,
    key_cache,
    value_cache,
    cache_len,
    attn_out_w,
    norm_gain,
    routes,
    gate_weights,
    w_gate,
    w_up,
    w_down,
):
    f32, bf16 = jnp.float32, jnp.bfloat16
    rows = hidden_in.shape[0]
    width = hidden_in.shape[1]
    quarter = width // 4
    replica = lax.axis_index("replica")
    x = lax.axis_index("expert") % LINE

    proj = jnp.concatenate([attn_out_w] + [from_x(attn_out_w, s) for s in range(1, LINE)], axis=0)
    proj = jnp.concatenate([proj, swap_core(proj)], axis=1)
    gate_mats = (w_gate[0], swap_core(w_gate)[0])
    up_mats = (w_up[0], swap_core(w_up)[0])
    down_mats = (w_down[0], swap_core(w_down)[0])

    hid = relative([hidden_in[:, q * quarter : (q + 1) * quarter] for q in range(4)], replica)
    hid_here = jnp.concatenate(hid[:2], axis=1)
    hid_there = swap_y(jnp.concatenate(hid[2:], axis=1))
    hid = jnp.concatenate([hid_here, hid_there], axis=0).astype(f32)
    gain = relative([norm_gain[q * quarter : (q + 1) * quarter] for q in range(4)], replica)
    gain = jnp.concatenate(gain[:2])

    expert = lax.axis_index("expert")

    def of_four(value):
        value = jnp.stack([value, swap_y(value)])
        return jnp.stack([value, swap_plane(value)], axis=1)

    route4, weight4 = of_four(routes), of_four(gate_weights)
    flat = route4.reshape(2, 2, rows * TOP)
    onehot = (flat[..., None] == jnp.arange(EXPERTS)).astype(jnp.int32)
    rank = jnp.sum((jnp.cumsum(onehot, axis=2) - 1) * onehot, axis=3).reshape(route4.shape)
    dz, dx = (route4 // 4 - expert // 4) % 4, (route4 - expert) % 4
    place = ((dz + dx) % 2 * 8 + dz * 2 + dx // 2) * 16 + rank
    place = place + CAP * jnp.arange(2)[None, :, None, None]
    place = jnp.where(route4 // 16 == expert // 16, place, -1).reshape(2, 2 * rows, TOP)
    chosen = place[..., None] == jnp.arange(EXPERTS * CAP)
    placing = jnp.any(chosen, axis=2).astype(bf16).transpose(0, 2, 1)
    weighting = jnp.sum(jnp.where(chosen, weight4.reshape(2, 2 * rows, TOP, 1), 0.0), axis=2)
    high = lax.reduce_precision(weighting, 8, 7)
    middle = lax.reduce_precision(weighting - high, 8, 7)
    weighting = jnp.concatenate([high, middle, weighting - high - middle], axis=1).astype(bf16)

    attn = attend_local(query, key_new, value_new, key_cache, value_cache, cache_len)
    heads = attn.reshape(rows, GROUPS, LINE, -1)
    heads = lax.dynamic_slice_in_dim(jnp.concatenate([heads, heads], axis=2), x, LINE, axis=2)
    heads = heads.reshape(rows, GROUPS, -1).transpose(1, 0, 2)
    heads = same_x(heads)
    heads = jnp.stack([heads, swap_y(heads)], axis=1)
    part = jnp.dot(heads.reshape(GROUPS * 2 * rows, -1), proj, preferred_element_type=f32)
    part = same_x(part.astype(bf16).reshape(GROUPS, 2 * rows, 2 * quarter))
    mid = hid + jnp.sum(part.astype(f32), axis=0)

    here, there = moe(mid, gain[None, :], placing, weighting, gate_mats, up_mats, down_mats)
    return jnp.concatenate(
        relative(
            (here[:, :quarter], here[:, quarter:], there[:, :quarter], there[:, quarter:]), replica
        ),
        axis=1,
    )


def solution(mesh):
    placed = (
        P(("replica", "expert"), None),
        P(("replica", "expert"), None),
        P(("replica", "expert"), None),
        P(("replica", "expert"), None),
        P(("replica", "expert"), None, None, None),
        P(("replica", "expert"), None, None, None),
        P(("replica", "expert")),
        P("expert", "replica"),
        P(),
        P(("replica", "expert"), None),
        P(("replica", "expert"), None),
        P("expert", "replica", None),
        P("expert", "replica", None),
        P("expert", None, "replica"),
    )
    return jax.shard_map(
        body, mesh=mesh, in_specs=placed, out_specs=P(("replica", "expert"), None), check_vma=False
    )
```

```python
import types

import jax
import jax.numpy as jnp
from jax import lax
from jax.experimental import pallas as pl
from jax.experimental.pallas import tpu as pltpu
from jax.sharding import PartitionSpec as P

HD = 128
TOP = 8
EXPERTS = 32
CAP = 8
ROWS = 16
RING = 8
TILE = 512
MESH = pl.DeviceIdType.MESH


def offset(s):
    dz = s % 8 // 2
    return dz, 2 * (s % 2) + (dz + s // 8) % 2


def shifted(expert, s, sign):
    dz, dx = offset(s)
    plane, z, x = expert // 16, expert // 4 % 4, expert % 4
    return plane * 16 + (z + 4 + sign * dz) % 4 * 4 + (x + 4 + sign * dx) % 4


def group_shifted(expert, t, sign):
    plane, z, x = expert // 16, expert // 4 % 4, expert % 4
    return (plane + t // 4) % 2 * 16 + (z + 4 + sign * (t % 4)) % 4 * 4 + x


def remote(src, dst, send, recv, device):
    return pltpu.make_async_remote_copy(
        src_ref=src,
        dst_ref=dst,
        send_sem=send,
        recv_sem=recv,
        device_id=device,
        device_id_type=MESH,
    )


def columns(n):
    return pl.ds(pl.multiple_of(n * TILE, TILE), TILE)


def scores_row(s, r, slot):
    groups = s.k_ring.shape[1]
    heads = s.q_rows.shape[1] // groups
    for g in range(groups):
        mine = pl.ds(g * heads, heads)
        s.scores[slot, mine, :] = lax.dot_general(
            s.q_rows[r, mine, :].astype(jnp.bfloat16),
            s.k_ring[slot, g],
            (((1,), (1,)), ((), ())),
            preferred_element_type=jnp.float32,
        )


def softmax_row(refs, s, r, slot):
    f32, bf16 = jnp.float32, jnp.bfloat16
    groups = s.k_ring.shape[1]
    heads = s.q_rows.shape[1] // groups
    scale = HD ** (-0.5)
    live = lax.broadcasted_iota(jnp.int32, s.scores.shape[1:], 1) < refs.cache_len[r]
    cached = jnp.where(live, s.scores[slot] * scale, -jnp.inf)
    own = [
        jnp.sum(
            s.q_rows[r, g * heads : (g + 1) * heads, :] * s.k_new[r, g : g + 1, :],
            axis=-1,
            keepdims=True,
        )
        for g in range(groups)
    ]
    own = jnp.concatenate(own, axis=0) * scale
    highest = jnp.maximum(jnp.max(cached, axis=-1, keepdims=True), own)
    cached_exp = jnp.exp(cached - highest)
    own_exp = jnp.exp(own - highest)
    inverse = 1.0 / (jnp.sum(cached_exp, axis=-1, keepdims=True) + own_exp)
    s.probs[slot] = (cached_exp * inverse).astype(bf16)
    own_prob = (own_exp * inverse).astype(bf16).astype(f32)
    for g in range(groups):
        mine = pl.ds(g * heads, heads)
        s.own_part[slot, mine, :] = (
            own_prob[g * heads : (g + 1) * heads] * s.v_new[r, g : g + 1, :]
        )


def values_row(s, r, slot):
    groups = s.k_ring.shape[1]
    heads = s.q_rows.shape[1] // groups
    for g in range(groups):
        mine = pl.ds(g * heads, heads)
        mixed = jnp.dot(
            s.probs[slot, mine, :], s.v_ring[slot, g], preferred_element_type=jnp.float32
        )
        s.o_rows[r, mine, :] = mixed + s.own_part[slot, mine, :]


def layer_kernel(names, scratch_names, *all_refs):
    refs = types.SimpleNamespace(**dict(zip(names, all_refs)))
    s = types.SimpleNamespace(**dict(zip(scratch_names, all_refs[len(names) :])))
    f32, bf16 = jnp.float32, jnp.bfloat16
    replica, expert = lax.axis_index("replica"), lax.axis_index("expert")
    plane, z, x = expert // 16, expert // 4 % 4, expert % 4
    sibling = replica // 2 * 2 + (replica + 1) % 2
    other_replica, other_plane = (replica + 2) % 4, (expert + 16) % 32
    other_sibling = other_replica // 2 * 2 + (other_replica + 1) % 2
    beside, across = (other_replica, expert), (replica, other_plane)
    diagonal, core = (other_replica, other_plane), (sibling, expert)
    line = expert // 4 * 4
    right, left = (replica, line + (x + 1) % 4), (replica, line + (x + 3) % 4)
    hidden, quarter = s.v_gate.shape[2], s.v_gate.shape[1]
    half = 2 * quarter
    n_rows = refs.cache_len.shape[0]
    deep = refs.attn_out_w.shape[0]

    def load_keys(r, slot):
        return pltpu.make_async_copy(refs.key_cache.at[r], s.k_ring.at[slot], s.k_sem.at[slot])

    def load_values(r, slot):
        return pltpu.make_async_copy(refs.value_cache.at[r], s.v_ring.at[slot], s.v_sem.at[slot])

    def proj_rows(block, start=0, count=deep):
        return pl.ds(pl.multiple_of(block * deep + start, 16), count)

    loads = [
        pltpu.make_async_copy(src, dst, s.load_sem.at[i])
        for i, (src, dst) in enumerate(
            [
                (refs.attn_out_w, s.v_proj.at[0, proj_rows(x)]),
                (refs.w_gate.at[0], s.v_gate.at[0]),
                (refs.w_up.at[0], s.v_up.at[0]),
                (refs.w_down.at[0], s.v_down.at[0]),
            ]
        )
    ]
    for r in range(RING):
        load_keys(r, r).start()
    loads[0].start()
    for r in range(RING):
        load_values(r, r).start()

    barrier = pltpu.get_barrier_semaphore()

    def greet(device):
        pl.semaphore_signal(barrier, inc=1, device_id=device, device_id_type=MESH)

    @pl.loop(1, 16)
    def _(i):
        greet((replica, shifted(expert, i, 1)))

    @pl.loop(1, 8)
    def _(t):
        greet((replica, group_shifted(expert, t, 1)))

    @pl.loop(0, 8)
    def _(t):
        greet((other_replica, group_shifted(expert, t, 1)))

    greet(core)

    for h in range(refs.query.shape[1] // HD):
        s.q_rows[:, h, :] = refs.query[:, h * HD : (h + 1) * HD].astype(f32)
    for g in range(refs.key_new.shape[1] // HD):
        s.k_new[:, g, :] = refs.key_new[:, g * HD : (g + 1) * HD].astype(f32)
        s.v_new[:, g, :] = refs.value_new[:, g * HD : (g + 1) * HD].astype(f32)

    square = (ROWS, ROWS)
    row_of = lax.broadcasted_iota(jnp.int32, square, 0)
    column_of = lax.broadcasted_iota(jnp.int32, square, 1)
    unit_matrix = jnp.where(row_of == column_of, 1.0, 0.0).astype(bf16)

    def turned(value):
        return lax.dot_general(
            unit_matrix, value, (((1,), (1,)), ((), ())), preferred_element_type=f32
        )

    routes = turned(refs.routes[...].astype(f32).astype(bf16)).astype(jnp.int32)
    rest = refs.gate_weights[...]
    gate_weights = jnp.zeros((ROWS, TOP), f32)
    for _ in range(3):
        piece = rest.astype(bf16)
        gate_weights = gate_weights + turned(piece)
        rest = rest - piece.astype(f32)
    lane = lax.broadcasted_iota(jnp.int32, (ROWS, 128), 1)
    named = jnp.zeros((ROWS, 128), f32)
    weight = jnp.zeros((ROWS, 128), f32)
    for k in range(TOP):
        hit = routes[:, k : k + 1] == lane % EXPERTS
        named = named + jnp.where(hit, 1.0, 0.0)
        weight = weight + jnp.where(hit, gate_weights[:, k : k + 1], 0.0)
    rank = jnp.dot(
        jnp.where(column_of < row_of, 1.0, 0.0).astype(bf16), named.astype(bf16), preferred_element_type=f32
    )
    high = weight.astype(bf16).astype(f32)
    middle = (weight - high).astype(bf16).astype(f32)
    kind = lane // EXPERTS
    s.info[0] = jnp.where(
        kind == 0,
        jnp.where(named > 0.0, rank, -1.0),
        jnp.where(kind == 1, high, jnp.where(kind == 2, middle, weight - high - middle)),
    )

    def quarter_of(q):
        return pl.ds(pl.multiple_of(q * quarter, quarter), quarter)

    s.hid_out[:, :quarter] = refs.hidden_in[:, quarter_of(other_replica)]
    s.hid_out[:, quarter:] = refs.hidden_in[:, quarter_of(other_sibling)]
    s.mid[:16, :quarter] = refs.hidden_in[:, quarter_of(replica)].astype(f32)
    s.mid[:16, quarter:] = refs.hidden_in[:, quarter_of(sibling)].astype(f32)
    s.gain[:, :quarter] = refs.norm_gain[:, quarter_of(replica)]
    s.gain[:, quarter:] = refs.norm_gain[:, quarter_of(sibling)]

    pl.semaphore_wait(barrier, 31)

    own_rows = s.v_proj.at[0, proj_rows(x)]
    to_right = remote(refs.attn_out_w, own_rows, s.x_send.at[0], s.x_recv.at[0], right)
    to_left = remote(refs.attn_out_w, own_rows, s.x_send.at[1], s.x_recv.at[1], left)
    to_core = [
        remote(
            refs.attn_out_w, s.v_proj.at[1, proj_rows(x)], s.core_send.at[0], s.core_recv.at[0], core
        )
    ]
    for i, (src, dst) in enumerate(
        [(refs.w_gate, s.v_gate), (refs.w_up, s.v_up), (refs.w_down, s.v_down)]
    ):
        to_core.append(
            remote(src.at[0], dst.at[1], s.core_send.at[i + 1], s.core_recv.at[i + 1], core)
        )
    early = [
        remote(s.info.at[0], s.info.at[2], s.early_send.at[0], s.early_recv.at[0], beside),
        remote(s.info.at[0], s.info.at[1], s.early_send.at[1], s.early_recv.at[1], across),
        remote(s.info.at[0], s.info.at[3], s.early_send.at[2], s.early_recv.at[2], diagonal),
        remote(s.hid_out, s.hid_in, s.early_send.at[3], s.early_recv.at[3], beside),
    ]
    for copy in [to_right, to_left] + early + to_core[:1]:
        copy.start()

    for b in range(n_rows // RING):
        last_turn = b == n_rows // RING - 1

        @pl.loop(0, RING, unroll=2)
        def _(i):
            load_keys(b * RING + i, i).wait()
            scores_row(s, b * RING + i, i)

        if not last_turn:
            for i in range(RING):
                load_keys((b + 1) * RING + i, i).start()

        @pl.loop(0, RING, unroll=2)
        def _(i):
            softmax_row(refs, s, b * RING + i, i)

        @pl.loop(0, RING, unroll=2)
        def _(i):
            load_values(b * RING + i, i).wait()
            values_row(s, b * RING + i, i)

        if not last_turn:
            for i in range(RING):
                load_values((b + 1) * RING + i, i).start()

    for copy in to_core[1:]:
        copy.start()
    for load in loads[1:]:
        load.start()

    to_right.wait_recv()
    to_left.wait_recv()
    mid_left, mid_right = proj_rows((x + 3) % 4, 0, deep // 2), proj_rows((x + 1) % 4, deep // 2, deep // 2)
    onward = [
        remote(s.v_proj.at[0, mid_left], s.v_proj.at[0, mid_left], s.x_send.at[2], s.x_recv.at[2], right),
        remote(s.v_proj.at[0, mid_right], s.v_proj.at[0, mid_right], s.x_send.at[3], s.x_recv.at[3], left),
    ]
    for step, i in ((1, 4), (3, 5), (2, 6)):
        rows = proj_rows((x + step) % 4)
        to_core.append(
            remote(
                s.v_proj.at[0, rows], s.v_proj.at[1, rows], s.core_send.at[i], s.core_recv.at[i], core
            )
        )
    for copy in onward + to_core[4:6]:
        copy.start()

    for h in range(s.o_rows.shape[1]):
        s.attn[h // 8, :, h % 8 * HD : (h % 8 + 1) * HD] = s.o_rows[:, h, :].astype(bf16)

    def heads_copy(t, h):
        there = group_shifted(expert, t, 1)
        return remote(
            s.attn.at[there // 4],
            s.heads.at[t, pl.ds(h * ROWS, ROWS)],
            s.heads_send.at[t, h],
            s.heads_recv.at[t, h],
            (other_replica if h else replica, there),
        )

    heads_copy(0, 1).start()

    @pl.loop(1, 8)
    def _(t):
        heads_copy(t, 0).start()
        heads_copy(t, 1).start()

    s.heads[0, :ROWS, :] = s.attn[expert // 4]
    for copy in onward:
        copy.wait_recv()
    to_core[6].start()

    for copy in early:
        copy.wait_recv()
    s.mid[16:, :] = s.hid_in[...].astype(f32)
    slot = lax.broadcasted_iota(jnp.int32, (128, 256), 1)
    step = slot // 16
    dz = step % 8 // 2
    dx = 2 * (step % 2) + (dz + step // 8) % 2
    taker = plane * 16 + (z + dz) % 4 * 4 + (x + dx) % 4
    entry = lax.broadcasted_iota(jnp.int32, (128, 256), 0)
    slot32 = lax.broadcasted_iota(jnp.int32, (32, 256), 1)
    row32 = lax.broadcasted_iota(jnp.int32, (32, 256), 0)
    for h in range(2):
        infos = s.info[2 * h : 2 * h + 2].reshape(32, 128).astype(bf16)
        picked = [
            jnp.dot(
                infos,
                jnp.where(entry == taker + EXPERTS * i, 1.0, 0.0).astype(bf16),
                preferred_element_type=f32,
            )
            for i in range(4)
        ]
        hit = (picked[0] == (slot32 % CAP).astype(f32)) & (slot32 // CAP % 2 == row32 // ROWS)
        s.placing[h] = jnp.where(hit, 1.0, 0.0).astype(bf16)
        for i in range(3):
            s.weighting[h, 32 * i : 32 * i + 32, :] = jnp.where(hit, picked[i + 1], 0.0).astype(bf16)

    def sums_copy(t):
        return remote(
            s.sums.at[t],
            s.sums_in.at[t],
            s.sums_send.at[t],
            s.sums_recv.at[t],
            (replica, group_shifted(expert, t, -1)),
        )

    loads[0].wait()
    to_core[0].wait_recv()
    for copy in to_core[4:]:
        copy.wait_recv()
    heads_copy(0, 1).wait_recv()
    for c in range(2):

        @pl.loop(max(1, 4 * c), 4 * c + 4)
        def _(t):
            heads_copy(t, 0).wait_recv()
            heads_copy(t, 1).wait_recv()

        for q in range(2):

            @pl.loop(0, quarter // TILE)
            def _(n):
                value = jnp.dot(
                    s.heads[4 * c : 4 * c + 4].reshape(128, quarter),
                    s.v_proj[q, :, columns(n)],
                    preferred_element_type=f32,
                )
                at = pl.multiple_of(q * quarter + n * TILE, TILE)
                s.sums[4 * c : 4 * c + 4, :, pl.ds(at, TILE)] = value.astype(bf16).reshape(4, 32, TILE)

        @pl.loop(max(1, 4 * c), 4 * c + 4)
        def _(t):
            sums_copy(t).start()

    @pl.loop(1, 8)
    def _(t):
        sums_copy(t).wait_recv()

    @pl.loop(0, half // TILE)
    def _(n):
        total = s.mid[:, columns(n)] + s.sums[0, :, columns(n)].astype(f32)
        for t in range(1, 8):
            total = total + s.sums_in[t, :, columns(n)].astype(f32)
        s.mid[:, columns(n)] = total

    mid = s.mid[...]
    s.square_out[...] = jnp.broadcast_to(jnp.sum(mid * mid, axis=-1, keepdims=True), (32, 128))
    s.scaled[...] = (mid * s.gain[...]).astype(bf16)
    pre = [
        remote(s.square_out, s.square_in.at[i], s.pre_send.at[i], s.pre_recv.at[i], device)
        for i, device in enumerate((beside, across, diagonal))
    ]
    pre.append(remote(s.scaled, s.scaled_in, s.pre_send.at[3], s.pre_recv.at[3], across))
    for copy in (pre[3], pre[0], pre[1], pre[2]):
        copy.start()
    for copy in pre:
        copy.wait_recv()
    for h in range(2):
        here, there = pl.ds(16 * h, 16), pl.ds(16 * (1 - h), 16)
        width = 2.0 * half
        total = s.square_out[here, :1] + s.square_in[0, there, :1]
        normed = s.mid[here, :] * s.gain[...] * lax.rsqrt(total / width + 1e-06)
        s.rows_all[h, :16, :] = normed.astype(bf16)
        total = s.square_in[1, here, :1] + s.square_in[2, there, :1]
        normed = s.scaled_in[here, :].astype(f32) * lax.rsqrt(total / width + 1e-06)
        s.rows_all[h, 16:, :] = normed.astype(bf16)

    def dispatch(h, i):
        rows = pl.ds(pl.multiple_of(i * 16, 16), 16)
        return remote(
            s.outgoing.at[h, rows],
            s.block.at[h, rows],
            s.disp_send.at[h, i],
            s.disp_recv.at[h, i],
            (replica, shifted(expert, i, 1)),
        )

    for h in (1, 0):

        @pl.loop(0, half // TILE)
        def _(n):
            cols = pl.ds(pl.multiple_of(n * TILE, TILE), TILE)
            s.outgoing[h, :, cols] = lax.dot_general(
                s.placing[h],
                s.rows_all[h, :, cols],
                (((0,), (0,)), ((), ())),
                preferred_element_type=f32,
            ).astype(bf16)

        @pl.loop(1, 16)
        def _(i):
            dispatch(h, i).start()

        s.block[h, :16, :] = s.outgoing[h, :16, :]

    tiles = hidden // TILE

    def gate_up(h, start, count, n):
        rows, cols = pl.ds(start, count), columns(n)
        for which, mats in enumerate((s.v_gate, s.v_up)):
            yield which, jnp.dot(
                s.block[h, rows, :quarter], mats[0, :, cols], preferred_element_type=f32
            ) + jnp.dot(s.block[h, rows, quarter:], mats[1, :, cols], preferred_element_type=f32)

    def part_copy(c, n):
        return remote(
            s.part_out.at[c, n],
            s.part_in.at[c, n],
            s.part_send.at[c, n],
            s.part_recv.at[c, n],
            beside,
        )

    loads[1].wait()
    loads[2].wait()
    to_core[1].wait_recv()
    to_core[2].wait_recv()
    for c in range(2):

        @pl.loop(max(1, 8 * c), 8 * c + 8)
        def _(i):
            dispatch(1, i).wait_recv()

        @pl.loop(0, tiles)
        def _(n):
            for which, value in gate_up(1, 128 * c, 128, n):
                s.part_out[c, n, which] = value.astype(bf16)
            part_copy(c, n).start()

    @pl.loop(1, 16)
    def _(i):
        dispatch(0, i).wait_recv()

    @pl.loop(0, tiles)
    def _(n):
        for which, value in gate_up(0, 0, 256, n):
            s.part_own[n, which] = value

    def give_back(h, i):
        rows = pl.ds(pl.multiple_of(i * 16, 16), 16)
        return remote(
            s.result.at[h, rows],
            s.returned.at[h, rows],
            s.ret_send.at[h, i],
            s.ret_recv.at[h, i],
            (replica, shifted(expert, i, -1)),
        )

    def down(h, c):
        for q in range(2):

            @pl.loop(0, quarter // TILE)
            def _(n):
                value = jnp.zeros((128, TILE), f32)
                for k in range(tiles):
                    value = value + jnp.dot(
                        s.units[h, c, k],
                        s.v_down[q, k * TILE : (k + 1) * TILE, columns(n)],
                        preferred_element_type=f32,
                    )
                at = pl.multiple_of(q * quarter + n * TILE, TILE)
                s.result[h, pl.ds(128 * c, 128), pl.ds(at, TILE)] = value.astype(bf16)

        @pl.loop(max(1, 8 * c), 8 * c + 8)
        def _(i):
            give_back(h, i).start()

        if c == 0:
            s.returned[h, :16, :] = s.result[h, :16, :]

    def unit_copy(c, n):
        return remote(
            s.units.at[0, c, n],
            s.units.at[1, c, n],
            s.unit_send.at[c, n],
            s.unit_recv.at[c, n],
            beside,
        )

    def combine(h, c):
        @pl.loop(max(1, 8 * c), 8 * c + 8)
        def _(i):
            give_back(h, i).wait_recv()

        @pl.loop(0, half // TILE)
        def _(n):
            three = jnp.dot(
                s.weighting[h, :, 128 * c : 128 * c + 128],
                s.returned[h, 128 * c : 128 * c + 128, columns(n)],
                preferred_element_type=f32,
            )
            value = three[:32] + three[32:64] + three[64:]
            s.mixed[h, :, columns(n)] = value if c == 0 else s.mixed[h, :, columns(n)] + value

    for c in range(2):

        @pl.loop(0, tiles)
        def _(n):
            part_copy(c, n).wait_recv()
            rows = pl.ds(128 * c, 128)
            gate = s.part_own[n, 0, rows, :] + s.part_in[c, n, 0].astype(f32)
            up_val = s.part_own[n, 1, rows, :] + s.part_in[c, n, 1].astype(f32)
            s.units[0, c, n] = (gate / (1.0 + jnp.exp(-gate)) * up_val).astype(bf16)
            unit_copy(c, n).start()

        if c == 0:
            loads[3].wait()
            to_core[3].wait_recv()
        down(0, c)
    last = [
        remote(s.last_out.at[i], s.last_in.at[i], s.last_send.at[i], s.last_recv.at[i], device)
        for i, device in enumerate((across, beside, diagonal))
    ]
    for c in range(2):

        @pl.loop(0, tiles)
        def _(n):
            unit_copy(c, n).wait_recv()

        down(1, c)
        if c == 0:
            combine(0, 0)
            combine(0, 1)
            s.last_out[0] = s.mixed[0, 16:, :].astype(bf16)
            last[0].start()
            combine(1, 0)
    combine(1, 1)
    s.last_out[1] = (s.mid[16:, :] + s.mixed[1, :16, :]).astype(bf16)
    s.last_out[2] = s.mixed[1, 16:, :].astype(bf16)
    last[1].start()
    last[2].start()
    for copy in last:
        copy.wait_recv()
    here = s.mid[:16, :] + s.mixed[0, :16, :]
    refs.near_sum[:, quarter_of(replica)] = here[:, :quarter]
    refs.near_sum[:, quarter_of(sibling)] = here[:, quarter:]
    there = s.last_in[1].astype(f32)
    refs.near_sum[:, quarter_of(other_replica)] = there[:, :quarter]
    refs.near_sum[:, quarter_of(other_sibling)] = there[:, quarter:]
    refs.far_sum[:, quarter_of(replica)] = s.last_in[0, :, :quarter]
    refs.far_sum[:, quarter_of(sibling)] = s.last_in[0, :, quarter:]
    refs.far_sum[:, quarter_of(other_replica)] = s.last_in[2, :, :quarter]
    refs.far_sum[:, quarter_of(other_sibling)] = s.last_in[2, :, quarter:]

    heads_copy(0, 1).wait_send()

    @pl.loop(1, 8)
    def _(t):
        heads_copy(t, 0).wait_send()
        heads_copy(t, 1).wait_send()
        sums_copy(t).wait_send()

    for copy in [to_right, to_left] + early + to_core + onward + pre + last:
        copy.wait_send()
    for h in range(2):

        @pl.loop(1, 16)
        def _(i):
            dispatch(h, i).wait_send()
            give_back(h, i).wait_send()

    for c in range(2):

        @pl.loop(0, tiles)
        def _(n):
            part_copy(c, n).wait_send()
            unit_copy(c, n).wait_send()


ARGS = (
    "hidden_in",
    "query",
    "key_new",
    "value_new",
    "key_cache",
    "value_cache",
    "cache_len",
    "attn_out_w",
    "norm_gain",
    "routes",
    "gate_weights",
    "w_gate",
    "w_up",
    "w_down",
)


def body(*args):
    f32, bf16 = jnp.float32, jnp.bfloat16
    given = dict(zip(ARGS, args))
    given["norm_gain"] = given["norm_gain"][None, :]
    given["routes"], given["gate_weights"] = given["routes"].T, given["gate_weights"].T
    n_rows, width = given["hidden_in"].shape
    groups, context, head_size = given["key_cache"].shape[1:]
    heads = given["query"].shape[1] // head_size
    _, quarter, hidden = given["w_gate"].shape
    deep = given["attn_out_w"].shape[0]
    half, tiles = 2 * quarter, hidden // TILE
    vmem, anywhere = pl.BlockSpec(memory_space=pltpu.VMEM), pl.BlockSpec(memory_space=pl.ANY)
    places = {name: vmem for name in ARGS}
    for name in ("key_cache", "value_cache", "attn_out_w", "w_gate", "w_up", "w_down"):
        places[name] = anywhere
    places["cache_len"] = pl.BlockSpec(memory_space=pltpu.SMEM)
    scratch = dict(
        k_ring=((RING, groups, context, head_size), bf16),
        v_ring=((RING, groups, context, head_size), bf16),
        q_rows=((n_rows, heads, head_size), f32),
        o_rows=((n_rows, heads, head_size), f32),
        scores=((RING, heads, context), f32),
        probs=((RING, heads, context), bf16),
        own_part=((RING, heads, head_size), f32),
        k_new=((n_rows, groups, head_size), f32),
        v_new=((n_rows, groups, head_size), f32),
        info=((4, ROWS, 128), f32),
        hid_out=((ROWS, half), bf16),
        hid_in=((ROWS, half), bf16),
        mid=((32, half), f32),
        gain=((1, half), f32),
        v_proj=((2, 4 * deep, quarter), bf16),
        v_gate=((2, quarter, hidden), bf16),
        v_up=((2, quarter, hidden), bf16),
        v_down=((2, hidden, quarter), bf16),
        attn=((8, ROWS, quarter), bf16),
        heads=((8, 32, quarter), bf16),
        sums=((8, 32, half), bf16),
        sums_in=((8, 32, half), bf16),
        placing=((2, 32, 256), bf16),
        weighting=((2, 96, 256), bf16),
        square_out=((32, 128), f32),
        square_in=((3, 32, 128), f32),
        scaled=((32, half), bf16),
        scaled_in=((32, half), bf16),
        rows_all=((2, 32, half), bf16),
        outgoing=((2, 256, half), bf16),
        block=((2, 256, half), bf16),
        part_out=((2, tiles, 2, 128, TILE), bf16),
        part_in=((2, tiles, 2, 128, TILE), bf16),
        part_own=((tiles, 2, 256, TILE), f32),
        units=((2, 2, tiles, 128, TILE), bf16),
        result=((2, 256, half), bf16),
        returned=((2, 256, half), bf16),
        mixed=((2, 32, half), f32),
        last_out=((3, 16, half), bf16),
        last_in=((3, 16, half), bf16),
    )
    semaphores = dict(
        k_sem=(RING,),
        v_sem=(RING,),
        load_sem=(4,),
        x_send=(4,),
        x_recv=(4,),
        core_send=(7,),
        core_recv=(7,),
        early_send=(4,),
        early_recv=(4,),
        heads_send=(8, 2),
        heads_recv=(8, 2),
        sums_send=(8,),
        sums_recv=(8,),
        pre_send=(4,),
        pre_recv=(4,),
        disp_send=(2, 16),
        disp_recv=(2, 16),
        part_send=(2, tiles),
        part_recv=(2, tiles),
        unit_send=(2, tiles),
        unit_recv=(2, tiles),
        ret_send=(2, 16),
        ret_recv=(2, 16),
        last_send=(3,),
        last_recv=(3,),
    )
    names = ARGS + ("near_sum", "far_sum")
    scratch_names = list(scratch) + list(semaphores)

    def kernel(*all_refs):
        layer_kernel(names, scratch_names, *all_refs)

    near_sum, far_sum = pl.pallas_call(
        kernel,
        out_shape=(
            jax.ShapeDtypeStruct((n_rows, width), f32),
            jax.ShapeDtypeStruct((n_rows, width), bf16),
        ),
        in_specs=[places[name] for name in ARGS],
        out_specs=(vmem, vmem),
        scratch_shapes=[pltpu.VMEM(*v) for v in scratch.values()]
        + [pltpu.SemaphoreType.DMA(v) for v in semaphores.values()],
        compiler_params=pltpu.CompilerParams(
            collective_id=0, has_side_effects=True, vmem_limit_bytes=60 * 1024 * 1024
        ),
        cost_estimate=pl.CostEstimate(
            flops=12 * 10**9, bytes_accessed=40 * 10**6, transcendentals=10**6
        ),
    )(*given.values())
    return (near_sum + far_sum.astype(f32)).astype(bf16)


def solution(mesh):
    placed = (
        P(("replica", "expert"), None),
        P(("replica", "expert"), None),
        P(("replica", "expert"), None),
        P(("replica", "expert"), None),
        P(("replica", "expert"), None, None, None),
        P(("replica", "expert"), None, None, None),
        P(("replica", "expert")),
        P("expert", "replica"),
        P(),
        P(("replica", "expert"), None),
        P(("replica", "expert"), None),
        P("expert", "replica", None),
        P("expert", "replica", None),
        P("expert", None, "replica"),
    )
    return jax.shard_map(
        body, mesh=mesh, in_specs=placed, out_specs=P(("replica", "expert"), None), check_vma=False
    )
```

```python
import types

import jax
import jax.numpy as jnp
from jax import lax
from jax.experimental import pallas as pl
from jax.experimental.pallas import tpu as pltpu
from jax.sharding import PartitionSpec as P

HD = 128
TOP = 8
EXPERTS = 32
CAP = 8
ROWS = 16
RING = 8
TILE = 512
CHUNKS = ((0, 8), (8, 8))
SHARES = ((0, 8), (8, 4), (12, 4))
MESH = pl.DeviceIdType.MESH


def offset(s):
    dz = s % 8 // 2
    return dz, 2 * (s % 2) + (dz + s // 8) % 2


def shifted(expert, s, sign):
    dz, dx = offset(s)
    plane, z, x = expert // 16, expert // 4 % 4, expert % 4
    return plane * 16 + (z + 4 + sign * dz) % 4 * 4 + (x + 4 + sign * dx) % 4


def group_shifted(expert, t, sign):
    plane, z, x = expert // 16, expert // 4 % 4, expert % 4
    return (plane + t // 4) % 2 * 16 + (z + 4 + sign * (t % 4)) % 4 * 4 + x


def remote(src, dst, send, recv, device):
    return pltpu.make_async_remote_copy(
        src_ref=src,
        dst_ref=dst,
        send_sem=send,
        recv_sem=recv,
        device_id=device,
        device_id_type=MESH,
    )


def columns(n):
    return pl.ds(pl.multiple_of(n * TILE, TILE), TILE)


def scores_row(s, r, slot):
    groups = s.k_ring.shape[1]
    heads = s.q_rows.shape[1] // groups
    for g in range(groups):
        mine = pl.ds(g * heads, heads)
        s.scores[slot, mine, :] = lax.dot_general(
            s.q_rows[r, mine, :].astype(jnp.bfloat16),
            s.k_ring[slot, g],
            (((1,), (1,)), ((), ())),
            preferred_element_type=jnp.float32,
        )


def softmax_row(refs, s, r, slot):
    f32, bf16 = jnp.float32, jnp.bfloat16
    groups = s.k_ring.shape[1]
    heads = s.q_rows.shape[1] // groups
    scale = HD ** (-0.5)
    live = lax.broadcasted_iota(jnp.int32, s.scores.shape[1:], 1) < refs.cache_len[r]
    cached = jnp.where(live, s.scores[slot] * scale, -jnp.inf)
    own = [
        jnp.sum(
            s.q_rows[r, g * heads : (g + 1) * heads, :] * s.k_new[r, g : g + 1, :],
            axis=-1,
            keepdims=True,
        )
        for g in range(groups)
    ]
    own = jnp.concatenate(own, axis=0) * scale
    highest = jnp.maximum(jnp.max(cached, axis=-1, keepdims=True), own)
    cached_exp = jnp.exp(cached - highest)
    own_exp = jnp.exp(own - highest)
    inverse = 1.0 / (jnp.sum(cached_exp, axis=-1, keepdims=True) + own_exp)
    s.probs[slot] = (cached_exp * inverse).astype(bf16)
    own_prob = (own_exp * inverse).astype(bf16).astype(f32)
    for g in range(groups):
        mine = pl.ds(g * heads, heads)
        s.own_part[slot, mine, :] = (
            own_prob[g * heads : (g + 1) * heads] * s.v_new[r, g : g + 1, :]
        )


def values_row(s, r, slot):
    groups = s.k_ring.shape[1]
    heads = s.q_rows.shape[1] // groups
    for g in range(groups):
        mine = pl.ds(g * heads, heads)
        mixed = jnp.dot(
            s.probs[slot, mine, :], s.v_ring[slot, g], preferred_element_type=jnp.float32
        )
        s.o_rows[r, mine, :] = mixed + s.own_part[slot, mine, :]


def layer_kernel(names, scratch_names, *all_refs):
    refs = types.SimpleNamespace(**dict(zip(names, all_refs)))
    s = types.SimpleNamespace(**dict(zip(scratch_names, all_refs[len(names) :])))
    f32, bf16 = jnp.float32, jnp.bfloat16
    replica, expert = lax.axis_index("replica"), lax.axis_index("expert")
    plane, z, x = expert // 16, expert // 4 % 4, expert % 4
    sibling = replica // 2 * 2 + (replica + 1) % 2
    other_replica, other_plane = (replica + 2) % 4, (expert + 16) % 32
    other_sibling = other_replica // 2 * 2 + (other_replica + 1) % 2
    beside, across = (other_replica, expert), (replica, other_plane)
    diagonal, core = (other_replica, other_plane), (sibling, expert)
    line = expert // 4 * 4
    right, left = (replica, line + (x + 1) % 4), (replica, line + (x + 3) % 4)
    hidden, quarter = s.v_gate.shape[2], s.v_gate.shape[1]
    half = 2 * quarter
    n_rows = refs.cache_len.shape[0]
    deep = refs.attn_out_w.shape[0]

    def load_keys(r, slot):
        return pltpu.make_async_copy(refs.key_cache.at[r], s.k_ring.at[slot], s.k_sem.at[slot])

    def load_values(r, slot):
        return pltpu.make_async_copy(refs.value_cache.at[r], s.v_ring.at[slot], s.v_sem.at[slot])

    def proj_rows(block, start=0, count=deep):
        return pl.ds(pl.multiple_of(block * deep + start, 16), count)

    loads = [
        pltpu.make_async_copy(src, dst, s.load_sem.at[i])
        for i, (src, dst) in enumerate(
            [
                (refs.attn_out_w, s.v_proj.at[0, proj_rows(x)]),
                (refs.w_gate.at[0], s.v_gate.at[0]),
                (refs.w_up.at[0], s.v_up.at[0]),
                (refs.w_down.at[0], s.v_down.at[0]),
            ]
        )
    ]
    for r in range(RING):
        load_keys(r, r).start()
    loads[0].start()
    for r in range(RING):
        load_values(r, r).start()

    barrier = pltpu.get_barrier_semaphore()

    def greet(device):
        pl.semaphore_signal(barrier, inc=1, device_id=device, device_id_type=MESH)

    @pl.loop(1, 16)
    def _(i):
        greet((replica, shifted(expert, i, 1)))

    @pl.loop(1, 8)
    def _(t):
        greet((replica, group_shifted(expert, t, 1)))

    @pl.loop(0, 8)
    def _(t):
        greet((other_replica, group_shifted(expert, t, 1)))

    greet(core)

    for h in range(refs.query.shape[1] // HD):
        s.q_rows[:, h, :] = refs.query[:, h * HD : (h + 1) * HD].astype(f32)
    for g in range(refs.key_new.shape[1] // HD):
        s.k_new[:, g, :] = refs.key_new[:, g * HD : (g + 1) * HD].astype(f32)
        s.v_new[:, g, :] = refs.value_new[:, g * HD : (g + 1) * HD].astype(f32)

    def quarter_of(q):
        return pl.ds(pl.multiple_of(q * quarter, quarter), quarter)

    pl.semaphore_wait(barrier, 31)

    half_deep = deep // 2

    def x_copy(i, block, part, device):
        rows = proj_rows(block, part * half_deep, half_deep)
        src = refs.attn_out_w.at[pl.ds(part * half_deep, half_deep)] if i < 4 else s.v_proj.at[0, rows]
        return remote(src, s.v_proj.at[0, rows], s.x_send.at[i], s.x_recv.at[i], device)

    along = [
        x_copy(0, x, 0, right),
        x_copy(1, x, 1, left),
        x_copy(2, x, 1, right),
        x_copy(3, x, 0, left),
    ]
    to_core = [
        remote(
            refs.attn_out_w, s.v_proj.at[1, proj_rows(x)], s.core_send.at[0], s.core_recv.at[0], core
        )
    ]
    for i, (src, dst) in enumerate(
        [(refs.w_gate, s.v_gate), (refs.w_up, s.v_up), (refs.w_down, s.v_down)]
    ):
        to_core.append(
            remote(src.at[0], dst.at[1], s.core_send.at[i + 1], s.core_recv.at[i + 1], core)
        )
    early = [
        remote(s.info.at[0], s.info.at[2], s.early_send.at[0], s.early_recv.at[0], beside),
        remote(s.info.at[0], s.info.at[1], s.early_send.at[1], s.early_recv.at[1], across),
        remote(s.info.at[0], s.info.at[3], s.early_send.at[2], s.early_recv.at[2], diagonal),
        remote(s.hid_out, s.hid_in, s.early_send.at[3], s.early_recv.at[3], beside),
    ]
    for copy in along + to_core[:1]:
        copy.start()

    square = (ROWS, ROWS)
    row_of = lax.broadcasted_iota(jnp.int32, square, 0)
    column_of = lax.broadcasted_iota(jnp.int32, square, 1)
    unit_matrix = jnp.where(row_of == column_of, 1.0, 0.0).astype(bf16)

    def turned(value):
        return lax.dot_general(
            unit_matrix, value, (((1,), (1,)), ((), ())), preferred_element_type=f32
        )

    routes = turned(refs.routes[...].astype(f32).astype(bf16)).astype(jnp.int32)
    rest = refs.gate_weights[...]
    gate_weights = jnp.zeros((ROWS, TOP), f32)
    for _ in range(3):
        piece = rest.astype(bf16)
        gate_weights = gate_weights + turned(piece)
        rest = rest - piece.astype(f32)
    lane = lax.broadcasted_iota(jnp.int32, (ROWS, 128), 1)
    named = jnp.zeros((ROWS, 128), f32)
    weight = jnp.zeros((ROWS, 128), f32)
    for k in range(TOP):
        hit = routes[:, k : k + 1] == lane % EXPERTS
        named = named + jnp.where(hit, 1.0, 0.0)
        weight = weight + jnp.where(hit, gate_weights[:, k : k + 1], 0.0)
    rank = jnp.dot(
        jnp.where(column_of < row_of, 1.0, 0.0).astype(bf16), named.astype(bf16), preferred_element_type=f32
    )
    high = weight.astype(bf16).astype(f32)
    middle = (weight - high).astype(bf16).astype(f32)
    kind = lane // EXPERTS
    s.info[0] = jnp.where(
        kind == 0,
        jnp.where(named > 0.0, rank, -1.0),
        jnp.where(kind == 1, high, jnp.where(kind == 2, middle, weight - high - middle)),
    )

    s.hid_out[:, :quarter] = refs.hidden_in[:, quarter_of(other_replica)]
    s.hid_out[:, quarter:] = refs.hidden_in[:, quarter_of(other_sibling)]
    s.mid[:16, :quarter] = refs.hidden_in[:, quarter_of(replica)].astype(f32)
    s.mid[:16, quarter:] = refs.hidden_in[:, quarter_of(sibling)].astype(f32)
    s.gain[:, :quarter] = refs.norm_gain[:, quarter_of(replica)]
    s.gain[:, quarter:] = refs.norm_gain[:, quarter_of(sibling)]
    for copy in early:
        copy.start()

    for b in range(n_rows // RING):
        last_turn = b == n_rows // RING - 1

        @pl.loop(0, RING, unroll=2)
        def _(i):
            load_keys(b * RING + i, i).wait()
            scores_row(s, b * RING + i, i)

        if not last_turn:
            for i in range(RING):
                load_keys((b + 1) * RING + i, i).start()

        @pl.loop(0, RING, unroll=2)
        def _(i):
            softmax_row(refs, s, b * RING + i, i)

        @pl.loop(0, RING, unroll=2)
        def _(i):
            load_values(b * RING + i, i).wait()
            values_row(s, b * RING + i, i)

        if not last_turn:
            for i in range(RING):
                load_values((b + 1) * RING + i, i).start()
        if b == 0:
            along[0].wait_recv()
            along[1].wait_recv()
            onward = [
                x_copy(4, (x + 3) % 4, 0, right),
                x_copy(5, (x + 1) % 4, 1, left),
            ]
            for copy in onward:
                copy.start()


    for h in range(s.o_rows.shape[1]):
        s.attn[h // 8, :, h % 8 * HD : (h % 8 + 1) * HD] = s.o_rows[:, h, :].astype(bf16)

    def heads_copy(h, t):
        there = group_shifted(expert, t, 1)
        return remote(
            s.attn.at[there // 4],
            s.heads.at[h, t],
            s.heads_send.at[h, t],
            s.heads_recv.at[h, t],
            (other_replica if h else replica, there),
        )

    for h in (1, 0):

        @pl.loop(1 - h, 8)
        def _(t):
            heads_copy(h, t).start()

    s.heads[0, 0] = s.attn[expert // 4]

    for copy in along[2:]:
        copy.wait_recv()
    for copy in onward:
        copy.wait_recv()
    for i, step in enumerate((1, 3, 2)):
        rows = proj_rows((x + step) % 4)
        to_core.append(
            remote(
                s.v_proj.at[0, rows],
                s.v_proj.at[1, rows],
                s.core_send.at[i + 4],
                s.core_recv.at[i + 4],
                core,
            )
        )
        to_core[-1].start()

    for copy in to_core[1:4]:
        copy.start()
    for load in loads[1:]:
        load.start()

    for copy in early:
        copy.wait_recv()
    s.mid[16:, :] = s.hid_in[...].astype(f32)
    slot = lax.broadcasted_iota(jnp.int32, (128, 256), 1)
    step = slot // 16
    dz = step % 8 // 2
    dx = 2 * (step % 2) + (dz + step // 8) % 2
    taker = plane * 16 + (z + dz) % 4 * 4 + (x + dx) % 4
    entry = lax.broadcasted_iota(jnp.int32, (128, 256), 0)
    slot32 = lax.broadcasted_iota(jnp.int32, (32, 256), 1)
    row32 = lax.broadcasted_iota(jnp.int32, (32, 256), 0)
    for h in range(2):
        infos = s.info[2 * h : 2 * h + 2].reshape(32, 128).astype(bf16)
        picked = [
            jnp.dot(
                infos,
                jnp.where(entry == taker + EXPERTS * i, 1.0, 0.0).astype(bf16),
                preferred_element_type=f32,
            )
            for i in range(4)
        ]
        hit = (picked[0] == (slot32 % CAP).astype(f32)) & (slot32 // CAP % 2 == row32 // ROWS)
        s.placing[h] = jnp.where(hit, 1.0, 0.0).astype(bf16)
        for i in range(3):
            s.weighting[h, 32 * i : 32 * i + 32, :] = jnp.where(hit, picked[i + 1], 0.0).astype(bf16)

    def sums_copy(h, t):
        return remote(
            s.sums.at[h, t],
            s.sums_in.at[h, t],
            s.sums_send.at[h, t],
            s.sums_recv.at[h, t],
            (replica, group_shifted(expert, t, -1)),
        )

    loads[0].wait()
    to_core[0].wait_recv()
    for copy in to_core[4:]:
        copy.wait_recv()
    for h in (1, 0):

        @pl.loop(1 - h, 8)
        def _(t):
            heads_copy(h, t).wait_recv()

        for q in range(2):

            @pl.loop(0, quarter // TILE)
            def _(n):
                value = jnp.dot(
                    s.heads[h].reshape(8 * ROWS, quarter),
                    s.v_proj[q, :, columns(n)],
                    preferred_element_type=f32,
                )
                at = pl.multiple_of(q * quarter + n * TILE, TILE)
                s.sums[h, :, :, pl.ds(at, TILE)] = value.astype(bf16).reshape(8, ROWS, TILE)

        @pl.loop(1, 8)
        def _(t):
            sums_copy(h, t).start()

    over = [
        remote(
            s.rows_all.at[h, pl.ds(0, ROWS)],
            s.rows_all.at[h, pl.ds(ROWS, ROWS)],
            s.over_send.at[h],
            s.over_recv.at[h],
            across,
        )
        for h in range(2)
    ]

    def finish_rows(h):
        @pl.loop(1, 8)
        def _(t):
            sums_copy(h, t).wait_recv()

        rows = pl.ds(ROWS * h, ROWS)

        @pl.loop(0, half // TILE)
        def _(n):
            total = s.mid[rows, columns(n)] + s.sums[h, 0, :, columns(n)].astype(f32)
            for t in range(1, 8):
                total = total + s.sums_in[h, t, :, columns(n)].astype(f32)
            s.mid[rows, columns(n)] = total
            s.rows_all[h, :ROWS, columns(n)] = (total * s.gain[:, columns(n)]).astype(bf16)

        over[h].start()
        mid = s.mid[rows, :]
        s.square_out[rows, :] = jnp.broadcast_to(
            jnp.sum(mid * mid, axis=-1, keepdims=True), (ROWS, 128)
        )

    def dispatch(h, i):
        rows = pl.ds(pl.multiple_of(i * 16, 16), 16)
        return remote(
            s.outgoing.at[h, rows],
            s.block.at[h, rows],
            s.disp_send.at[h, i],
            s.disp_recv.at[h, i],
            (replica, shifted(expert, i, 1)),
        )

    def send_rows(h):
        over[h].wait_recv()
        for first, number in CHUNKS:
            slots = pl.ds(16 * first, 16 * number)

            @pl.loop(0, half // TILE)
            def _(n):
                s.outgoing[h, slots, columns(n)] = lax.dot_general(
                    s.placing[h, :, slots],
                    s.rows_all[h, :, columns(n)],
                    (((0,), (0,)), ((), ())),
                    preferred_element_type=f32,
                ).astype(bf16)

            @pl.loop(max(1, first), first + number)
            def _(i):
                dispatch(h, i).start()

            if first == 0:
                s.block[h, :16, :] = s.outgoing[h, :16, :]

    finish_rows(1)
    send_rows(1)
    finish_rows(0)
    squares = [
        remote(
            s.square_out, s.square_in.at[i], s.square_send.at[i], s.square_recv.at[i], device
        )
        for i, device in enumerate((beside, across, diagonal))
    ]
    for copy in squares:
        copy.start()
    send_rows(0)

    def scale_copy(i):
        slots = pl.ds(pl.multiple_of(i * 16, 16), 16)
        return remote(
            s.scale_out.at[slots],
            s.scale_in.at[slots],
            s.scale_send.at[i],
            s.scale_recv.at[i],
            (replica, shifted(expert, i, 1)),
        )

    def send_scales():
        for copy in squares:
            copy.wait_recv()
        total = jnp.concatenate(
            [
                s.square_out[:ROWS, :] + s.square_in[0, ROWS:, :],
                s.square_in[1, :ROWS, :] + s.square_in[2, ROWS:, :],
            ],
            axis=0,
        )
        rest = lax.rsqrt(total / (2.0 * half) + 1e-06)
        value = jnp.zeros((256, 128), f32)
        for _ in range(3):
            piece = rest.astype(bf16)
            value = value + lax.dot_general(
                s.placing[0], piece, (((0,), (0,)), ((), ())), preferred_element_type=f32
            )
            rest = rest - piece.astype(f32)
        s.scale_out[...] = value

        @pl.loop(1, 16)
        def _(i):
            scale_copy(i).start()

        s.scale_in[:16, :] = value[:16]

    tiles = hidden // TILE

    def slots_of(c, chunks=CHUNKS):
        first, number = chunks[c]
        return pl.ds(16 * first, 16 * number)

    def gate_up(h, c, n):
        for which, mats in enumerate((s.v_gate, s.v_up)):
            yield which, jnp.dot(
                s.block[h, slots_of(c), :quarter],
                mats[0, :, columns(n)],
                preferred_element_type=f32,
            ) + jnp.dot(
                s.block[h, slots_of(c), quarter:],
                mats[1, :, columns(n)],
                preferred_element_type=f32,
            )

    def part_copy(c, n):
        return remote(
            s.part_out.at[n, :, slots_of(c)],
            s.part_in.at[n, :, slots_of(c)],
            s.part_send.at[c, n],
            s.part_recv.at[c, n],
            beside,
        )

    def wait_rows(h, c):
        first, number = CHUNKS[c]

        @pl.loop(max(1, first), first + number)
        def _(i):
            dispatch(h, i).wait_recv()

    loads[1].wait()
    loads[2].wait()
    to_core[1].wait_recv()
    to_core[2].wait_recv()
    for c in range(len(CHUNKS)):
        wait_rows(1, c)

        @pl.loop(0, tiles)
        def _(n):
            for which, value in gate_up(1, c, n):
                s.part_out[n, which, slots_of(c), :] = value.astype(bf16)
            part_copy(c, n).start()

        if c == 0:
            send_scales()

    def own_part(c):
        wait_rows(0, c)

        @pl.loop(0, tiles)
        def _(n):
            for which, value in gate_up(0, c, n):
                s.part_own[n, which, slots_of(c), :] = value

    def give_back(h, i):
        rows = pl.ds(pl.multiple_of(i * 16, 16), 16)
        return remote(
            s.result.at[h, rows],
            s.returned.at[h, rows],
            s.ret_send.at[h, i],
            s.ret_recv.at[h, i],
            (replica, shifted(expert, i, -1)),
        )

    def down(h, c, chunks):
        first, number = chunks[c]
        for q in range(2):

            @pl.loop(0, quarter // TILE)
            def _(n):
                value = jnp.zeros((16 * number, TILE), f32)
                for k in range(tiles):
                    value = value + jnp.dot(
                        s.units[h, k, slots_of(c, chunks), :],
                        s.v_down[q, k * TILE : (k + 1) * TILE, columns(n)],
                        preferred_element_type=f32,
                    )
                at = pl.multiple_of(q * quarter + n * TILE, TILE)
                s.result[h, slots_of(c, chunks), pl.ds(at, TILE)] = value.astype(bf16)

        @pl.loop(max(1, first), first + number)
        def _(i):
            give_back(h, i).start()

        if first == 0:
            s.returned[h, :16, :] = s.result[h, :16, :]

    def unit_copy(c, n):
        return remote(
            s.units.at[0, n, slots_of(c, SHARES)],
            s.units.at[1, n, slots_of(c, SHARES)],
            s.unit_send.at[c, n],
            s.unit_recv.at[c, n],
            beside,
        )

    def combine(h, begin, end):
        @pl.loop(max(1, begin), end)
        def _(i):
            give_back(h, i).wait_recv()

        slots = pl.ds(16 * begin, 16 * (end - begin))

        @pl.loop(0, half // TILE)
        def _(n):
            three = jnp.dot(
                s.weighting[h, :, slots],
                s.returned[h, slots, columns(n)],
                preferred_element_type=f32,
            )
            value = three[:32] + three[32:64] + three[64:]
            s.mixed[h, :, columns(n)] = value if begin == 0 else s.mixed[h, :, columns(n)] + value

    @pl.loop(1, 16)
    def _(i):
        scale_copy(i).wait_recv()

    own_part(0)
    for c in range(len(CHUNKS)):

        @pl.loop(0, tiles)
        def _(n):
            part_copy(c, n).wait_recv()
            scale = s.scale_in[slots_of(c), :1]
            gate = s.part_own[n, 0, slots_of(c), :] + s.part_in[n, 0, slots_of(c), :].astype(f32)
            up_val = s.part_own[n, 1, slots_of(c), :] + s.part_in[n, 1, slots_of(c), :].astype(f32)
            gate, up_val = gate * scale, up_val * scale
            s.units[0, n, slots_of(c), :] = (gate / (1.0 + jnp.exp(-gate)) * up_val).astype(bf16)
            unit_copy(c, n).start()

        if c == 1:

            @pl.loop(0, tiles)
            def _(n):
                unit_copy(2, n).start()

        if c == 0:
            loads[3].wait()
            to_core[3].wait_recv()
        if c + 1 < len(CHUNKS):
            own_part(c + 1)
        down(0, c, CHUNKS)
    last = [
        remote(s.last_out.at[i], s.last_in.at[i], s.last_send.at[i], s.last_recv.at[i], device)
        for i, device in enumerate((across, beside, diagonal))
    ]
    for c in range(len(SHARES)):

        @pl.loop(0, tiles)
        def _(n):
            unit_copy(c, n).wait_recv()

        down(1, c, SHARES)
        if c == 0:
            combine(0, 0, 16)
            s.last_out[0] = s.mixed[0, 16:, :].astype(bf16)
            last[0].start()
            combine(1, 0, 8)
    combine(1, 8, 12)
    combine(1, 12, 16)
    s.last_out[1] = (s.mid[16:, :] + s.mixed[1, :16, :]).astype(bf16)
    s.last_out[2] = s.mixed[1, 16:, :].astype(bf16)
    last[1].start()
    last[2].start()
    for copy in last:
        copy.wait_recv()
    here = s.mid[:16, :] + s.mixed[0, :16, :]
    refs.near_sum[:, quarter_of(replica)] = here[:, :quarter]
    refs.near_sum[:, quarter_of(sibling)] = here[:, quarter:]
    there = s.last_in[1].astype(f32)
    refs.near_sum[:, quarter_of(other_replica)] = there[:, :quarter]
    refs.near_sum[:, quarter_of(other_sibling)] = there[:, quarter:]
    refs.far_sum[:, quarter_of(replica)] = s.last_in[0, :, :quarter]
    refs.far_sum[:, quarter_of(sibling)] = s.last_in[0, :, quarter:]
    refs.far_sum[:, quarter_of(other_replica)] = s.last_in[2, :, :quarter]
    refs.far_sum[:, quarter_of(other_sibling)] = s.last_in[2, :, quarter:]

    for copy in along + early + to_core + onward + over + squares + last:
        copy.wait_send()
    for h in range(2):

        @pl.loop(1 - h, 8)
        def _(t):
            heads_copy(h, t).wait_send()

        @pl.loop(1, 8)
        def _(t):
            sums_copy(h, t).wait_send()

        @pl.loop(1, 16)
        def _(i):
            dispatch(h, i).wait_send()
            give_back(h, i).wait_send()

    @pl.loop(1, 16)
    def _(i):
        scale_copy(i).wait_send()

    for c in range(len(CHUNKS)):

        @pl.loop(0, tiles)
        def _(n):
            part_copy(c, n).wait_send()

    for c in range(len(SHARES)):

        @pl.loop(0, tiles)
        def _(n):
            unit_copy(c, n).wait_send()


ARGS = (
    "hidden_in",
    "query",
    "key_new",
    "value_new",
    "key_cache",
    "value_cache",
    "cache_len",
    "attn_out_w",
    "norm_gain",
    "routes",
    "gate_weights",
    "w_gate",
    "w_up",
    "w_down",
)


def body(*args):
    f32, bf16 = jnp.float32, jnp.bfloat16
    given = dict(zip(ARGS, args))
    given["norm_gain"] = given["norm_gain"][None, :]
    given["routes"], given["gate_weights"] = given["routes"].T, given["gate_weights"].T
    n_rows, width = given["hidden_in"].shape
    groups, context, head_size = given["key_cache"].shape[1:]
    heads = given["query"].shape[1] // head_size
    _, quarter, hidden = given["w_gate"].shape
    deep = given["attn_out_w"].shape[0]
    half, tiles = 2 * quarter, hidden // TILE
    vmem, anywhere = pl.BlockSpec(memory_space=pltpu.VMEM), pl.BlockSpec(memory_space=pl.ANY)
    places = {name: vmem for name in ARGS}
    for name in ("key_cache", "value_cache", "attn_out_w", "w_gate", "w_up", "w_down"):
        places[name] = anywhere
    places["cache_len"] = pl.BlockSpec(memory_space=pltpu.SMEM)
    scratch = dict(
        k_ring=((RING, groups, context, head_size), bf16),
        v_ring=((RING, groups, context, head_size), bf16),
        q_rows=((n_rows, heads, head_size), f32),
        o_rows=((n_rows, heads, head_size), f32),
        scores=((RING, heads, context), f32),
        probs=((RING, heads, context), bf16),
        own_part=((RING, heads, head_size), f32),
        k_new=((n_rows, groups, head_size), f32),
        v_new=((n_rows, groups, head_size), f32),
        info=((4, ROWS, 128), f32),
        hid_out=((ROWS, half), bf16),
        hid_in=((ROWS, half), bf16),
        mid=((32, half), f32),
        gain=((1, half), f32),
        v_proj=((2, 4 * deep, quarter), bf16),
        v_gate=((2, quarter, hidden), bf16),
        v_up=((2, quarter, hidden), bf16),
        v_down=((2, hidden, quarter), bf16),
        attn=((8, ROWS, quarter), bf16),
        heads=((2, 8, ROWS, quarter), bf16),
        sums=((2, 8, ROWS, half), bf16),
        sums_in=((2, 8, ROWS, half), bf16),
        placing=((2, 32, 256), bf16),
        weighting=((2, 96, 256), bf16),
        square_out=((32, 128), f32),
        square_in=((3, 32, 128), f32),
        scale_out=((256, 128), f32),
        scale_in=((256, 128), f32),
        rows_all=((2, 32, half), bf16),
        outgoing=((2, 256, half), bf16),
        block=((2, 256, half), bf16),
        part_out=((tiles, 2, 256, TILE), bf16),
        part_in=((tiles, 2, 256, TILE), bf16),
        part_own=((tiles, 2, 256, TILE), f32),
        units=((2, tiles, 256, TILE), bf16),
        result=((2, 256, half), bf16),
        returned=((2, 256, half), bf16),
        mixed=((2, 32, half), f32),
        last_out=((3, 16, half), bf16),
        last_in=((3, 16, half), bf16),
    )
    semaphores = dict(
        k_sem=(RING,),
        v_sem=(RING,),
        load_sem=(4,),
        x_send=(6,),
        x_recv=(6,),
        core_send=(7,),
        core_recv=(7,),
        early_send=(4,),
        early_recv=(4,),
        heads_send=(2, 8),
        heads_recv=(2, 8),
        sums_send=(2, 8),
        sums_recv=(2, 8),
        over_send=(2,),
        over_recv=(2,),
        square_send=(3,),
        square_recv=(3,),
        scale_send=(16,),
        scale_recv=(16,),
        disp_send=(2, 16),
        disp_recv=(2, 16),
        part_send=(len(CHUNKS), tiles),
        part_recv=(len(CHUNKS), tiles),
        unit_send=(len(SHARES), tiles),
        unit_recv=(len(SHARES), tiles),
        ret_send=(2, 16),
        ret_recv=(2, 16),
        last_send=(3,),
        last_recv=(3,),
    )
    names = ARGS + ("near_sum", "far_sum")
    scratch_names = list(scratch) + list(semaphores)

    def kernel(*all_refs):
        layer_kernel(names, scratch_names, *all_refs)

    near_sum, far_sum = pl.pallas_call(
        kernel,
        out_shape=(
            jax.ShapeDtypeStruct((n_rows, width), f32),
            jax.ShapeDtypeStruct((n_rows, width), bf16),
        ),
        in_specs=[places[name] for name in ARGS],
        out_specs=(vmem, vmem),
        scratch_shapes=[pltpu.VMEM(*v) for v in scratch.values()]
        + [pltpu.SemaphoreType.DMA(v) for v in semaphores.values()],
        compiler_params=pltpu.CompilerParams(
            collective_id=0, has_side_effects=True, vmem_limit_bytes=60 * 1024 * 1024
        ),
        cost_estimate=pl.CostEstimate(
            flops=12 * 10**9, bytes_accessed=40 * 10**6, transcendentals=10**6
        ),
    )(*given.values())
    return (near_sum + far_sum.astype(f32)).astype(bf16)


def solution(mesh):
    placed = (
        P(("replica", "expert"), None),
        P(("replica", "expert"), None),
        P(("replica", "expert"), None),
        P(("replica", "expert"), None),
        P(("replica", "expert"), None, None, None),
        P(("replica", "expert"), None, None, None),
        P(("replica", "expert")),
        P("expert", "replica"),
        P(),
        P(("replica", "expert"), None),
        P(("replica", "expert"), None),
        P("expert", "replica", None),
        P("expert", "replica", None),
        P("expert", None, "replica"),
    )
    return jax.shard_map(
        body, mesh=mesh, in_specs=placed, out_specs=P(("replica", "expert"), None), check_vma=False
    )
```

```python
import types

import jax
import jax.numpy as jnp
from jax import lax
from jax.experimental import pallas as pl
from jax.experimental.pallas import tpu as pltpu
from jax.sharding import PartitionSpec as P

HD = 128
TOP = 8
EXPERTS = 32
CAP = 8
ROWS = 16
RING = 8
TILE = 512
CHUNKS = ((0, 8), (8, 8))
SHARES = ((0, 8), (8, 4), (12, 4))
MESH = pl.DeviceIdType.MESH


def offset(s):
    dz = s % 8 // 2
    return dz, 2 * (s % 2) + (dz + s // 8) % 2


def shifted(expert, s, sign):
    dz, dx = offset(s)
    plane, z, x = expert // 16, expert // 4 % 4, expert % 4
    return plane * 16 + (z + 4 + sign * dz) % 4 * 4 + (x + 4 + sign * dx) % 4


def group_shifted(expert, t, sign):
    plane, z, x = expert // 16, expert // 4 % 4, expert % 4
    return (plane + t // 4) % 2 * 16 + (z + 4 + sign * (t % 4)) % 4 * 4 + x


def remote(src, dst, send, recv, device):
    return pltpu.make_async_remote_copy(
        src_ref=src,
        dst_ref=dst,
        send_sem=send,
        recv_sem=recv,
        device_id=device,
        device_id_type=MESH,
    )


def columns(n):
    return pl.ds(pl.multiple_of(n * TILE, TILE), TILE)


def scores_row(s, r, slot):
    groups = s.k_ring.shape[1]
    heads = s.q_rows.shape[1] // groups
    for g in range(groups):
        mine = pl.ds(g * heads, heads)
        s.scores[slot, mine, :] = lax.dot_general(
            s.q_rows[r, mine, :].astype(jnp.bfloat16),
            s.k_ring[slot, g],
            (((1,), (1,)), ((), ())),
            preferred_element_type=jnp.float32,
        )


def softmax_row(refs, s, r, slot):
    f32, bf16 = jnp.float32, jnp.bfloat16
    groups = s.k_ring.shape[1]
    heads = s.q_rows.shape[1] // groups
    scale = HD ** (-0.5)
    live = lax.broadcasted_iota(jnp.int32, s.scores.shape[1:], 1) < refs.cache_len[r]
    cached = jnp.where(live, s.scores[slot] * scale, -jnp.inf)
    own = [
        jnp.sum(
            s.q_rows[r, g * heads : (g + 1) * heads, :] * s.k_new[r, g : g + 1, :],
            axis=-1,
            keepdims=True,
        )
        for g in range(groups)
    ]
    own = jnp.concatenate(own, axis=0) * scale
    highest = jnp.maximum(jnp.max(cached, axis=-1, keepdims=True), own)
    cached_exp = jnp.exp(cached - highest)
    own_exp = jnp.exp(own - highest)
    inverse = 1.0 / (jnp.sum(cached_exp, axis=-1, keepdims=True) + own_exp)
    s.probs[slot] = (cached_exp * inverse).astype(bf16)
    own_prob = (own_exp * inverse).astype(bf16).astype(f32)
    for g in range(groups):
        mine = pl.ds(g * heads, heads)
        s.own_part[slot, mine, :] = (
            own_prob[g * heads : (g + 1) * heads] * s.v_new[r, g : g + 1, :]
        )


def values_row(s, r, slot):
    groups = s.k_ring.shape[1]
    heads = s.q_rows.shape[1] // groups
    for g in range(groups):
        mine = pl.ds(g * heads, heads)
        mixed = jnp.dot(
            s.probs[slot, mine, :], s.v_ring[slot, g], preferred_element_type=jnp.float32
        )
        s.o_rows[r, mine, :] = mixed + s.own_part[slot, mine, :]


def layer_kernel(names, scratch_names, *all_refs):
    refs = types.SimpleNamespace(**dict(zip(names, all_refs)))
    s = types.SimpleNamespace(**dict(zip(scratch_names, all_refs[len(names) :])))
    f32, bf16 = jnp.float32, jnp.bfloat16
    replica, expert = lax.axis_index("replica"), lax.axis_index("expert")
    plane, z, x = expert // 16, expert // 4 % 4, expert % 4
    sibling = replica // 2 * 2 + (replica + 1) % 2
    other_replica, other_plane = (replica + 2) % 4, (expert + 16) % 32
    other_sibling = other_replica // 2 * 2 + (other_replica + 1) % 2
    beside, across = (other_replica, expert), (replica, other_plane)
    diagonal, core = (other_replica, other_plane), (sibling, expert)
    line = expert // 4 * 4
    right, left = (replica, line + (x + 1) % 4), (replica, line + (x + 3) % 4)
    hidden, quarter = s.v_gate.shape[2], s.v_gate.shape[1]
    half = 2 * quarter
    n_rows = refs.cache_len.shape[0]
    deep = refs.attn_out_w.shape[0]

    barrier = pltpu.get_barrier_semaphore()

    def greet(device):
        pl.semaphore_signal(barrier, inc=1, device_id=device, device_id_type=MESH)

    @pl.loop(1, 16)
    def _(i):
        greet((replica, shifted(expert, i, 1)))

    @pl.loop(1, 8)
    def _(t):
        greet((replica, group_shifted(expert, t, 1)))

    @pl.loop(0, 8)
    def _(t):
        greet((other_replica, group_shifted(expert, t, 1)))

    greet(core)

    small = [
        pltpu.make_async_copy(getattr(refs, name), getattr(s, "in_" + name), s.small_sem.at[i])
        for i, name in enumerate(SMALL)
    ]
    for copy in small:
        copy.start()

    def load_keys(r, slot):
        return pltpu.make_async_copy(refs.key_cache.at[r], s.k_ring.at[slot], s.k_sem.at[slot])

    def load_values(r, slot):
        return pltpu.make_async_copy(refs.value_cache.at[r], s.v_ring.at[slot], s.v_sem.at[slot])

    def proj_rows(block, start=0, count=deep):
        return pl.ds(pl.multiple_of(block * deep + start, 16), count)

    loads = [
        pltpu.make_async_copy(src, dst, s.load_sem.at[i])
        for i, (src, dst) in enumerate(
            [
                (refs.attn_out_w, s.v_proj.at[0, proj_rows(x)]),
                (refs.w_gate.at[0], s.v_gate.at[0]),
                (refs.w_up.at[0], s.v_up.at[0]),
                (refs.w_down.at[0], s.v_down.at[0]),
            ]
        )
    ]
    for r in range(RING):
        load_keys(r, r).start()
    loads[0].start()
    for r in range(RING):
        load_values(r, r).start()

    def quarter_of(q):
        return pl.ds(pl.multiple_of(q * quarter, quarter), quarter)

    pl.semaphore_wait(barrier, 31)

    half_deep = deep // 2

    def x_copy(i, block, part, device):
        rows = proj_rows(block, part * half_deep, half_deep)
        src = refs.attn_out_w.at[pl.ds(part * half_deep, half_deep)] if i < 4 else s.v_proj.at[0, rows]
        return remote(src, s.v_proj.at[0, rows], s.x_send.at[i], s.x_recv.at[i], device)

    along = [
        x_copy(0, x, 0, right),
        x_copy(1, x, 1, left),
        x_copy(2, x, 1, right),
        x_copy(3, x, 0, left),
    ]
    to_core = [
        remote(
            refs.attn_out_w, s.v_proj.at[1, proj_rows(x)], s.core_send.at[0], s.core_recv.at[0], core
        )
    ]
    for i, (src, dst) in enumerate(
        [(refs.w_gate, s.v_gate), (refs.w_up, s.v_up), (refs.w_down, s.v_down)]
    ):
        to_core.append(
            remote(src.at[0], dst.at[1], s.core_send.at[i + 1], s.core_recv.at[i + 1], core)
        )
    early = [
        remote(s.info.at[0], s.info.at[2], s.early_send.at[0], s.early_recv.at[0], beside),
        remote(s.info.at[0], s.info.at[1], s.early_send.at[1], s.early_recv.at[1], across),
        remote(s.info.at[0], s.info.at[3], s.early_send.at[2], s.early_recv.at[2], diagonal),
        remote(s.hid_out, s.hid_in, s.early_send.at[3], s.early_recv.at[3], beside),
    ]
    for copy in along + to_core[:1]:
        copy.start()

    for copy in small:
        copy.wait()
    for h in range(s.in_query.shape[1] // HD):
        s.q_rows[:, h, :] = s.in_query[:, h * HD : (h + 1) * HD].astype(f32)
    for g in range(s.in_key_new.shape[1] // HD):
        s.k_new[:, g, :] = s.in_key_new[:, g * HD : (g + 1) * HD].astype(f32)
        s.v_new[:, g, :] = s.in_value_new[:, g * HD : (g + 1) * HD].astype(f32)

    square = (ROWS, ROWS)
    row_of = lax.broadcasted_iota(jnp.int32, square, 0)
    column_of = lax.broadcasted_iota(jnp.int32, square, 1)
    unit_matrix = jnp.where(row_of == column_of, 1.0, 0.0).astype(bf16)

    def turned(value):
        return lax.dot_general(
            unit_matrix, value, (((1,), (1,)), ((), ())), preferred_element_type=f32
        )

    routes = turned(s.in_routes[...].astype(f32).astype(bf16)).astype(jnp.int32)
    rest = s.in_gate_weights[...]
    gate_weights = jnp.zeros((ROWS, TOP), f32)
    for _ in range(3):
        piece = rest.astype(bf16)
        gate_weights = gate_weights + turned(piece)
        rest = rest - piece.astype(f32)
    lane = lax.broadcasted_iota(jnp.int32, (ROWS, 128), 1)
    named = jnp.zeros((ROWS, 128), f32)
    weight = jnp.zeros((ROWS, 128), f32)
    for k in range(TOP):
        hit = routes[:, k : k + 1] == lane % EXPERTS
        named = named + jnp.where(hit, 1.0, 0.0)
        weight = weight + jnp.where(hit, gate_weights[:, k : k + 1], 0.0)
    rank = jnp.dot(
        jnp.where(column_of < row_of, 1.0, 0.0).astype(bf16), named.astype(bf16), preferred_element_type=f32
    )
    high = weight.astype(bf16).astype(f32)
    middle = (weight - high).astype(bf16).astype(f32)
    kind = lane // EXPERTS
    s.info[0] = jnp.where(
        kind == 0,
        jnp.where(named > 0.0, rank, -1.0),
        jnp.where(kind == 1, high, jnp.where(kind == 2, middle, weight - high - middle)),
    )

    s.hid_out[:, :quarter] = s.in_hidden_in[:, quarter_of(other_replica)]
    s.hid_out[:, quarter:] = s.in_hidden_in[:, quarter_of(other_sibling)]
    s.mid[:16, :quarter] = s.in_hidden_in[:, quarter_of(replica)].astype(f32)
    s.mid[:16, quarter:] = s.in_hidden_in[:, quarter_of(sibling)].astype(f32)
    s.gain[:, :quarter] = s.in_norm_gain[:, quarter_of(replica)]
    s.gain[:, quarter:] = s.in_norm_gain[:, quarter_of(sibling)]
    for copy in early + to_core[1:2]:
        copy.start()

    for b in range(n_rows // RING):
        last_turn = b == n_rows // RING - 1

        @pl.loop(0, RING, unroll=2)
        def _(i):
            load_keys(b * RING + i, i).wait()
            scores_row(s, b * RING + i, i)

        if not last_turn:
            for i in range(RING):
                load_keys((b + 1) * RING + i, i).start()

        @pl.loop(0, RING, unroll=2)
        def _(i):
            softmax_row(refs, s, b * RING + i, i)

        @pl.loop(0, RING, unroll=2)
        def _(i):
            load_values(b * RING + i, i).wait()
            values_row(s, b * RING + i, i)

        if not last_turn:
            for i in range(RING):
                load_values((b + 1) * RING + i, i).start()
        if b == 0:
            along[0].wait_recv()
            along[1].wait_recv()
            onward = [
                x_copy(4, (x + 3) % 4, 0, right),
                x_copy(5, (x + 1) % 4, 1, left),
            ]
            for copy in onward + to_core[2:3]:
                copy.start()


    for h in range(s.o_rows.shape[1]):
        s.attn[h // 8, :, h % 8 * HD : (h % 8 + 1) * HD] = s.o_rows[:, h, :].astype(bf16)

    def heads_copy(h, t):
        there = group_shifted(expert, t, 1)
        return remote(
            s.attn.at[there // 4],
            s.heads.at[h, t],
            s.heads_send.at[h, t],
            s.heads_recv.at[h, t],
            (other_replica if h else replica, there),
        )

    for h in (1, 0):

        @pl.loop(1 - h, 8)
        def _(t):
            heads_copy(h, t).start()

    s.heads[0, 0] = s.attn[expert // 4]

    for copy in along[2:]:
        copy.wait_recv()
    for copy in onward:
        copy.wait_recv()
    for i, step in enumerate((1, 3, 2)):
        rows = proj_rows((x + step) % 4)
        to_core.append(
            remote(
                s.v_proj.at[0, rows],
                s.v_proj.at[1, rows],
                s.core_send.at[i + 4],
                s.core_recv.at[i + 4],
                core,
            )
        )
        to_core[-1].start()

    for load in loads[1:]:
        load.start()

    for copy in early:
        copy.wait_recv()
    s.mid[16:, :] = s.hid_in[...].astype(f32)
    slot = lax.broadcasted_iota(jnp.int32, (128, 256), 1)
    step = slot // 16
    dz = step % 8 // 2
    dx = 2 * (step % 2) + (dz + step // 8) % 2
    taker = plane * 16 + (z + dz) % 4 * 4 + (x + dx) % 4
    entry = lax.broadcasted_iota(jnp.int32, (128, 256), 0)
    slot32 = lax.broadcasted_iota(jnp.int32, (32, 256), 1)
    row32 = lax.broadcasted_iota(jnp.int32, (32, 256), 0)
    for h in range(2):
        infos = s.info[2 * h : 2 * h + 2].reshape(32, 128).astype(bf16)
        picked = [
            jnp.dot(
                infos,
                jnp.where(entry == taker + EXPERTS * i, 1.0, 0.0).astype(bf16),
                preferred_element_type=f32,
            )
            for i in range(4)
        ]
        hit = (picked[0] == (slot32 % CAP).astype(f32)) & (slot32 // CAP % 2 == row32 // ROWS)
        s.placing[h] = jnp.where(hit, 1.0, 0.0).astype(bf16)
        for i in range(3):
            s.weighting[h, 32 * i : 32 * i + 32, :] = jnp.where(hit, picked[i + 1], 0.0).astype(bf16)

    def sums_copy(h, t):
        return remote(
            s.sums.at[h, t],
            s.sums_in.at[h, t],
            s.sums_send.at[h, t],
            s.sums_recv.at[h, t],
            (replica, group_shifted(expert, t, -1)),
        )

    loads[0].wait()
    to_core[0].wait_recv()
    for copy in to_core[4:]:
        copy.wait_recv()
    to_core[3].start()
    for h in (1, 0):

        @pl.loop(1 - h, 8)
        def _(t):
            heads_copy(h, t).wait_recv()

        for q in range(2):

            @pl.loop(0, quarter // TILE)
            def _(n):
                value = jnp.dot(
                    s.heads[h].reshape(8 * ROWS, quarter),
                    s.v_proj[q, :, columns(n)],
                    preferred_element_type=f32,
                )
                at = pl.multiple_of(q * quarter + n * TILE, TILE)
                s.sums[h, :, :, pl.ds(at, TILE)] = value.astype(bf16).reshape(8, ROWS, TILE)

        @pl.loop(1, 8)
        def _(t):
            sums_copy(h, t).start()

    over = [
        remote(
            s.rows_all.at[h, pl.ds(0, ROWS)],
            s.rows_all.at[h, pl.ds(ROWS, ROWS)],
            s.over_send.at[h],
            s.over_recv.at[h],
            across,
        )
        for h in range(2)
    ]

    def finish_rows(h):
        @pl.loop(1, 8)
        def _(t):
            sums_copy(h, t).wait_recv()

        rows = pl.ds(ROWS * h, ROWS)

        @pl.loop(0, half // TILE)
        def _(n):
            total = s.mid[rows, columns(n)] + s.sums[h, 0, :, columns(n)].astype(f32)
            for t in range(1, 8):
                total = total + s.sums_in[h, t, :, columns(n)].astype(f32)
            s.mid[rows, columns(n)] = total
            s.rows_all[h, :ROWS, columns(n)] = (total * s.gain[:, columns(n)]).astype(bf16)

        over[h].start()
        mid = s.mid[rows, :]
        s.square_out[rows, :] = jnp.broadcast_to(
            jnp.sum(mid * mid, axis=-1, keepdims=True), (ROWS, 128)
        )

    def dispatch(h, i):
        rows = pl.ds(pl.multiple_of(i * 16, 16), 16)
        return remote(
            s.outgoing.at[h, rows],
            s.block.at[h, rows],
            s.disp_send.at[h, i],
            s.disp_recv.at[h, i],
            (replica, shifted(expert, i, 1)),
        )

    def send_rows(h, c):
        if c == 0:
            over[h].wait_recv()
        first, number = CHUNKS[c]
        slots = pl.ds(16 * first, 16 * number)

        @pl.loop(0, half // TILE)
        def _(n):
            s.outgoing[h, slots, columns(n)] = lax.dot_general(
                s.placing[h, :, slots],
                s.rows_all[h, :, columns(n)],
                (((0,), (0,)), ((), ())),
                preferred_element_type=f32,
            ).astype(bf16)

        @pl.loop(max(1, first), first + number)
        def _(i):
            dispatch(h, i).start()

        if first == 0:
            s.block[h, :16, :] = s.outgoing[h, :16, :]

    finish_rows(1)
    send_rows(1, 0)
    finish_rows(0)
    squares = [
        remote(
            s.square_out, s.square_in.at[i], s.square_send.at[i], s.square_recv.at[i], device
        )
        for i, device in enumerate((beside, across, diagonal))
    ]
    for copy in squares:
        copy.start()
    send_rows(1, 1)
    send_rows(0, 0)

    def scale_copy(i):
        slots = pl.ds(pl.multiple_of(i * 16, 16), 16)
        return remote(
            s.scale_out.at[slots],
            s.scale_in.at[slots],
            s.scale_send.at[i],
            s.scale_recv.at[i],
            (replica, shifted(expert, i, 1)),
        )

    def send_scales():
        for copy in squares:
            copy.wait_recv()
        total = jnp.concatenate(
            [
                s.square_out[:ROWS, :] + s.square_in[0, ROWS:, :],
                s.square_in[1, :ROWS, :] + s.square_in[2, ROWS:, :],
            ],
            axis=0,
        )
        rest = lax.rsqrt(total / (2.0 * half) + 1e-06)
        value = jnp.zeros((256, 128), f32)
        for _ in range(3):
            piece = rest.astype(bf16)
            value = value + lax.dot_general(
                s.placing[0], piece, (((0,), (0,)), ((), ())), preferred_element_type=f32
            )
            rest = rest - piece.astype(f32)
        s.scale_out[...] = value

        @pl.loop(1, 16)
        def _(i):
            scale_copy(i).start()

        s.scale_in[:16, :] = value[:16]

    tiles = hidden // TILE

    def slots_of(c, chunks=CHUNKS):
        first, number = chunks[c]
        return pl.ds(16 * first, 16 * number)

    def gate_up(h, c, n):
        for which, mats in enumerate((s.v_gate, s.v_up)):
            yield which, jnp.dot(
                s.block[h, slots_of(c), :quarter],
                mats[0, :, columns(n)],
                preferred_element_type=f32,
            ) + jnp.dot(
                s.block[h, slots_of(c), quarter:],
                mats[1, :, columns(n)],
                preferred_element_type=f32,
            )

    def part_copy(c, n):
        return remote(
            s.part_out.at[n, :, slots_of(c)],
            s.part_in.at[n, :, slots_of(c)],
            s.part_send.at[c, n],
            s.part_recv.at[c, n],
            beside,
        )

    def wait_rows(h, c):
        first, number = CHUNKS[c]

        @pl.loop(max(1, first), first + number)
        def _(i):
            dispatch(h, i).wait_recv()

    loads[1].wait()
    loads[2].wait()
    to_core[1].wait_recv()
    to_core[2].wait_recv()
    for c in range(len(CHUNKS)):
        wait_rows(1, c)

        @pl.loop(0, tiles)
        def _(n):
            for which, value in gate_up(1, c, n):
                s.part_out[n, which, slots_of(c), :] = value.astype(bf16)
            part_copy(c, n).start()

        if c == 0:
            send_rows(0, 1)
            send_scales()

    def own_part(c):
        wait_rows(0, c)

        @pl.loop(0, tiles)
        def _(n):
            for which, value in gate_up(0, c, n):
                s.part_own[n, which, slots_of(c), :] = value

    def give_back(h, i):
        rows = pl.ds(pl.multiple_of(i * 16, 16), 16)
        return remote(
            s.result.at[h, rows],
            s.returned.at[h, rows],
            s.ret_send.at[h, i],
            s.ret_recv.at[h, i],
            (replica, shifted(expert, i, -1)),
        )

    def down(h, c, chunks):
        first, number = chunks[c]
        for q in range(2):

            @pl.loop(0, quarter // TILE)
            def _(n):
                value = jnp.zeros((16 * number, TILE), f32)
                for k in range(tiles):
                    value = value + jnp.dot(
                        s.units[h, k, slots_of(c, chunks), :],
                        s.v_down[q, k * TILE : (k + 1) * TILE, columns(n)],
                        preferred_element_type=f32,
                    )
                at = pl.multiple_of(q * quarter + n * TILE, TILE)
                s.result[h, slots_of(c, chunks), pl.ds(at, TILE)] = value.astype(bf16)

        @pl.loop(max(1, first), first + number)
        def _(i):
            give_back(h, i).start()

        if first == 0:
            s.returned[h, :16, :] = s.result[h, :16, :]

    def unit_copy(c, n):
        return remote(
            s.units.at[0, n, slots_of(c, SHARES)],
            s.units.at[1, n, slots_of(c, SHARES)],
            s.unit_send.at[c, n],
            s.unit_recv.at[c, n],
            beside,
        )

    def combine(h, begin, end):
        @pl.loop(max(1, begin), end)
        def _(i):
            give_back(h, i).wait_recv()

        slots = pl.ds(16 * begin, 16 * (end - begin))

        @pl.loop(0, half // TILE)
        def _(n):
            three = jnp.dot(
                s.weighting[h, :, slots],
                s.returned[h, slots, columns(n)],
                preferred_element_type=f32,
            )
            value = three[:32] + three[32:64] + three[64:]
            s.mixed[h, :, columns(n)] = value if begin == 0 else s.mixed[h, :, columns(n)] + value

    @pl.loop(1, 16)
    def _(i):
        scale_copy(i).wait_recv()

    own_part(0)
    for c in range(len(CHUNKS)):

        @pl.loop(0, tiles)
        def _(n):
            part_copy(c, n).wait_recv()
            scale = s.scale_in[slots_of(c), :1]
            gate = s.part_own[n, 0, slots_of(c), :] + s.part_in[n, 0, slots_of(c), :].astype(f32)
            up_val = s.part_own[n, 1, slots_of(c), :] + s.part_in[n, 1, slots_of(c), :].astype(f32)
            gate, up_val = gate * scale, up_val * scale
            s.units[0, n, slots_of(c), :] = (gate / (1.0 + jnp.exp(-gate)) * up_val).astype(bf16)
            unit_copy(c, n).start()

        if c == 1:

            @pl.loop(0, tiles)
            def _(n):
                unit_copy(2, n).start()

        if c == 0:
            loads[3].wait()
            to_core[3].wait_recv()
        if c + 1 < len(CHUNKS):
            own_part(c + 1)
        down(0, c, CHUNKS)
    last = [
        remote(s.last_out.at[i], s.last_in.at[i], s.last_send.at[i], s.last_recv.at[i], device)
        for i, device in enumerate((across, beside, diagonal))
    ]
    for c in range(len(SHARES)):

        @pl.loop(0, tiles)
        def _(n):
            unit_copy(c, n).wait_recv()

        down(1, c, SHARES)
        if c == 1:
            combine(0, 0, 16)
            s.last_out[0] = s.mixed[0, 16:, :].astype(bf16)
            last[0].start()
    for copy in along + early + to_core + onward + over + squares:
        copy.wait_send()

    @pl.loop(1, 8)
    def _(i):
        heads_copy(0, i).wait_send()
        heads_copy(1, i).wait_send()
        sums_copy(0, i).wait_send()
        sums_copy(1, i).wait_send()
        give_back(1, i).wait_send()

    heads_copy(1, 0).wait_send()

    @pl.loop(1, 16)
    def _(i):
        dispatch(0, i).wait_send()
        dispatch(1, i).wait_send()
        scale_copy(i).wait_send()
        give_back(0, i).wait_send()

    @pl.loop(0, tiles)
    def _(n):
        part_copy(0, n).wait_send()
        part_copy(1, n).wait_send()
        unit_copy(0, n).wait_send()

    combine(1, 0, 8)
    combine(1, 8, 12)
    combine(1, 12, 16)
    s.last_out[1] = (s.mid[16:, :] + s.mixed[1, :16, :]).astype(bf16)
    s.last_out[2] = s.mixed[1, 16:, :].astype(bf16)
    last[1].start()
    last[2].start()
    for copy in last:
        copy.wait_recv()
    here = s.mid[:16, :] + s.mixed[0, :16, :]
    refs.near_sum[:, quarter_of(replica)] = here[:, :quarter]
    refs.near_sum[:, quarter_of(sibling)] = here[:, quarter:]
    there = s.last_in[1].astype(f32)
    refs.near_sum[:, quarter_of(other_replica)] = there[:, :quarter]
    refs.near_sum[:, quarter_of(other_sibling)] = there[:, quarter:]
    refs.far_sum[:, quarter_of(replica)] = s.last_in[0, :, :quarter]
    refs.far_sum[:, quarter_of(sibling)] = s.last_in[0, :, quarter:]
    refs.far_sum[:, quarter_of(other_replica)] = s.last_in[2, :, :quarter]
    refs.far_sum[:, quarter_of(other_sibling)] = s.last_in[2, :, quarter:]

    for copy in last:
        copy.wait_send()

    @pl.loop(8, 16)
    def _(i):
        give_back(1, i).wait_send()

    @pl.loop(0, tiles)
    def _(n):
        unit_copy(1, n).wait_send()
        unit_copy(2, n).wait_send()


ARGS = (
    "hidden_in",
    "query",
    "key_new",
    "value_new",
    "key_cache",
    "value_cache",
    "cache_len",
    "attn_out_w",
    "norm_gain",
    "routes",
    "gate_weights",
    "w_gate",
    "w_up",
    "w_down",
)


SMALL = (
    "query",
    "key_new",
    "value_new",
    "routes",
    "gate_weights",
    "hidden_in",
    "norm_gain",
)


def body(*args):
    f32, bf16 = jnp.float32, jnp.bfloat16
    given = dict(zip(ARGS, args))
    given["norm_gain"] = given["norm_gain"][None, :]
    given["routes"], given["gate_weights"] = given["routes"].T, given["gate_weights"].T
    n_rows, width = given["hidden_in"].shape
    groups, context, head_size = given["key_cache"].shape[1:]
    heads = given["query"].shape[1] // head_size
    _, quarter, hidden = given["w_gate"].shape
    deep = given["attn_out_w"].shape[0]
    half, tiles = 2 * quarter, hidden // TILE
    vmem, anywhere = pl.BlockSpec(memory_space=pltpu.VMEM), pl.BlockSpec(memory_space=pl.ANY)
    places = {name: anywhere for name in ARGS}
    places["cache_len"] = pl.BlockSpec(memory_space=pltpu.SMEM)
    scratch = {"in_" + name: (given[name].shape, given[name].dtype) for name in SMALL}
    scratch |= dict(
        k_ring=((RING, groups, context, head_size), bf16),
        v_ring=((RING, groups, context, head_size), bf16),
        q_rows=((n_rows, heads, head_size), f32),
        o_rows=((n_rows, heads, head_size), f32),
        scores=((RING, heads, context), f32),
        probs=((RING, heads, context), bf16),
        own_part=((RING, heads, head_size), f32),
        k_new=((n_rows, groups, head_size), f32),
        v_new=((n_rows, groups, head_size), f32),
        info=((4, ROWS, 128), f32),
        hid_out=((ROWS, half), bf16),
        hid_in=((ROWS, half), bf16),
        mid=((32, half), f32),
        gain=((1, half), f32),
        v_proj=((2, 4 * deep, quarter), bf16),
        v_gate=((2, quarter, hidden), bf16),
        v_up=((2, quarter, hidden), bf16),
        v_down=((2, hidden, quarter), bf16),
        attn=((8, ROWS, quarter), bf16),
        heads=((2, 8, ROWS, quarter), bf16),
        sums=((2, 8, ROWS, half), bf16),
        sums_in=((2, 8, ROWS, half), bf16),
        placing=((2, 32, 256), bf16),
        weighting=((2, 96, 256), bf16),
        square_out=((32, 128), f32),
        square_in=((3, 32, 128), f32),
        scale_out=((256, 128), f32),
        scale_in=((256, 128), f32),
        rows_all=((2, 32, half), bf16),
        outgoing=((2, 256, half), bf16),
        block=((2, 256, half), bf16),
        part_out=((tiles, 2, 256, TILE), bf16),
        part_in=((tiles, 2, 256, TILE), bf16),
        part_own=((tiles, 2, 256, TILE), f32),
        units=((2, tiles, 256, TILE), bf16),
        result=((2, 256, half), bf16),
        returned=((2, 256, half), bf16),
        mixed=((2, 32, half), f32),
        last_out=((3, 16, half), bf16),
        last_in=((3, 16, half), bf16),
    )
    semaphores = dict(
        k_sem=(RING,),
        v_sem=(RING,),
        load_sem=(4,),
        small_sem=(len(SMALL),),
        x_send=(6,),
        x_recv=(6,),
        core_send=(7,),
        core_recv=(7,),
        early_send=(4,),
        early_recv=(4,),
        heads_send=(2, 8),
        heads_recv=(2, 8),
        sums_send=(2, 8),
        sums_recv=(2, 8),
        over_send=(2,),
        over_recv=(2,),
        square_send=(3,),
        square_recv=(3,),
        scale_send=(16,),
        scale_recv=(16,),
        disp_send=(2, 16),
        disp_recv=(2, 16),
        part_send=(len(CHUNKS), tiles),
        part_recv=(len(CHUNKS), tiles),
        unit_send=(len(SHARES), tiles),
        unit_recv=(len(SHARES), tiles),
        ret_send=(2, 16),
        ret_recv=(2, 16),
        last_send=(3,),
        last_recv=(3,),
    )
    names = ARGS + ("near_sum", "far_sum")
    scratch_names = list(scratch) + list(semaphores)

    def kernel(*all_refs):
        layer_kernel(names, scratch_names, *all_refs)

    near_sum, far_sum = pl.pallas_call(
        kernel,
        out_shape=(
            jax.ShapeDtypeStruct((n_rows, width), f32),
            jax.ShapeDtypeStruct((n_rows, width), bf16),
        ),
        in_specs=[places[name] for name in ARGS],
        out_specs=(vmem, vmem),
        scratch_shapes=[pltpu.VMEM(*v) for v in scratch.values()]
        + [pltpu.SemaphoreType.DMA(v) for v in semaphores.values()],
        compiler_params=pltpu.CompilerParams(
            collective_id=0, has_side_effects=True, vmem_limit_bytes=60 * 1024 * 1024
        ),
        cost_estimate=pl.CostEstimate(
            flops=12 * 10**9, bytes_accessed=40 * 10**6, transcendentals=10**6
        ),
    )(*given.values())
    return (near_sum + far_sum.astype(f32)).astype(bf16)


def solution(mesh):
    placed = (
        P(("replica", "expert"), None),
        P(("replica", "expert"), None),
        P(("replica", "expert"), None),
        P(("replica", "expert"), None),
        P(("replica", "expert"), None, None, None),
        P(("replica", "expert"), None, None, None),
        P(("replica", "expert")),
        P("expert", "replica"),
        P(),
        P(("replica", "expert"), None),
        P(("replica", "expert"), None),
        P("expert", "replica", None),
        P("expert", "replica", None),
        P("expert", None, "replica"),
    )
    return jax.shard_map(
        body, mesh=mesh, in_specs=placed, out_specs=P(("replica", "expert"), None), check_vma=False
    )
```

```python
import types

import jax
import jax.numpy as jnp
from jax import lax
from jax.experimental import pallas as pl
from jax.experimental.pallas import tpu as pltpu
from jax.sharding import PartitionSpec as P

HD = 128
TOP = 8
EXPERTS = 32
CAP = 8
ROWS = 16
RING = 8
TILE = 512
CHUNKS = ((0, 8), (8, 8))
SHARES = ((0, 8), (8, 4), (12, 4))
MESH = pl.DeviceIdType.MESH


def offset(s):
    dz = s % 8 // 2
    return dz, 2 * (s % 2) + (dz + s // 8) % 2


def shifted(expert, s, sign):
    dz, dx = offset(s)
    plane, z, x = expert // 16, expert // 4 % 4, expert % 4
    return plane * 16 + (z + 4 + sign * dz) % 4 * 4 + (x + 4 + sign * dx) % 4


def group_shifted(expert, t, sign):
    plane, z, x = expert // 16, expert // 4 % 4, expert % 4
    return (plane + t // 4) % 2 * 16 + (z + 4 + sign * (t % 4)) % 4 * 4 + x


def remote(src, dst, send, recv, device):
    return pltpu.make_async_remote_copy(
        src_ref=src,
        dst_ref=dst,
        send_sem=send,
        recv_sem=recv,
        device_id=device,
        device_id_type=MESH,
    )


def columns(n):
    return pl.ds(pl.multiple_of(n * TILE, TILE), TILE)


def scores_row(s, r, slot):
    groups = s.k_ring.shape[1]
    heads = s.q_rows.shape[1] // groups
    for g in range(groups):
        mine = pl.ds(g * heads, heads)
        s.scores[slot, mine, :] = lax.dot_general(
            s.q_rows[r, mine, :].astype(jnp.bfloat16),
            s.k_ring[slot, g],
            (((1,), (1,)), ((), ())),
            preferred_element_type=jnp.float32,
        )


def softmax_row(refs, s, r, slot):
    f32, bf16 = jnp.float32, jnp.bfloat16
    groups = s.k_ring.shape[1]
    heads = s.q_rows.shape[1] // groups
    scale = HD ** (-0.5)
    live = lax.broadcasted_iota(jnp.int32, s.scores.shape[1:], 1) < refs.cache_len[r]
    cached = jnp.where(live, s.scores[slot] * scale, -jnp.inf)
    own = [
        jnp.sum(
            s.q_rows[r, g * heads : (g + 1) * heads, :] * s.k_new[r, g : g + 1, :],
            axis=-1,
            keepdims=True,
        )
        for g in range(groups)
    ]
    own = jnp.concatenate(own, axis=0) * scale
    highest = jnp.maximum(jnp.max(cached, axis=-1, keepdims=True), own)
    cached_exp = jnp.exp(cached - highest)
    own_exp = jnp.exp(own - highest)
    inverse = 1.0 / (jnp.sum(cached_exp, axis=-1, keepdims=True) + own_exp)
    s.probs[slot] = (cached_exp * inverse).astype(bf16)
    own_prob = (own_exp * inverse).astype(bf16).astype(f32)
    for g in range(groups):
        mine = pl.ds(g * heads, heads)
        s.own_part[slot, mine, :] = (
            own_prob[g * heads : (g + 1) * heads] * s.v_new[r, g : g + 1, :]
        )


def values_row(s, r, slot):
    groups = s.k_ring.shape[1]
    heads = s.q_rows.shape[1] // groups
    for g in range(groups):
        mine = pl.ds(g * heads, heads)
        mixed = jnp.dot(
            s.probs[slot, mine, :], s.v_ring[slot, g], preferred_element_type=jnp.float32
        )
        s.o_rows[r, mine, :] = mixed + s.own_part[slot, mine, :]


def layer_kernel(names, scratch_names, *all_refs):
    refs = types.SimpleNamespace(**dict(zip(names, all_refs)))
    s = types.SimpleNamespace(**dict(zip(scratch_names, all_refs[len(names) :])))
    f32, bf16 = jnp.float32, jnp.bfloat16
    replica, expert = lax.axis_index("replica"), lax.axis_index("expert")
    plane, z, x = expert // 16, expert // 4 % 4, expert % 4
    sibling = replica // 2 * 2 + (replica + 1) % 2
    other_replica, other_plane = (replica + 2) % 4, (expert + 16) % 32
    other_sibling = other_replica // 2 * 2 + (other_replica + 1) % 2
    beside, across = (other_replica, expert), (replica, other_plane)
    diagonal, core = (other_replica, other_plane), (sibling, expert)
    line = expert // 4 * 4
    right, left = (replica, line + (x + 1) % 4), (replica, line + (x + 3) % 4)
    hidden, quarter = s.v_gate.shape[2], s.v_gate.shape[1]
    half = 2 * quarter
    n_rows = refs.cache_len.shape[0]
    deep = refs.attn_out_w.shape[0]

    barrier = pltpu.get_barrier_semaphore()

    def greet(device):
        pl.semaphore_signal(barrier, inc=1, device_id=device, device_id_type=MESH)

    @pl.loop(1, 16)
    def _(i):
        greet((replica, shifted(expert, i, 1)))

    @pl.loop(1, 8)
    def _(t):
        greet((replica, group_shifted(expert, t, 1)))

    @pl.loop(0, 8)
    def _(t):
        greet((other_replica, group_shifted(expert, t, 1)))

    greet(core)

    small = [
        pltpu.make_async_copy(getattr(refs, name), getattr(s, "in_" + name), s.small_sem.at[i])
        for i, name in enumerate(SMALL)
    ]
    for copy in small:
        copy.start()

    def load_keys(r, slot):
        return pltpu.make_async_copy(refs.key_cache.at[r], s.k_ring.at[slot], s.k_sem.at[slot])

    def load_values(r, slot):
        return pltpu.make_async_copy(refs.value_cache.at[r], s.v_ring.at[slot], s.v_sem.at[slot])

    def proj_rows(block, start=0, count=deep):
        return pl.ds(pl.multiple_of(block * deep + start, 16), count)

    loads = [
        pltpu.make_async_copy(src, dst, s.load_sem.at[i])
        for i, (src, dst) in enumerate(
            [
                (refs.attn_out_w, s.v_proj.at[0, proj_rows(x)]),
                (refs.w_gate.at[0], s.v_gate.at[0]),
                (refs.w_up.at[0], s.v_up.at[0]),
                (refs.w_down.at[0], s.v_down.at[0]),
            ]
        )
    ]
    for r in range(RING):
        load_keys(r, r).start()
    loads[0].start()
    for r in range(RING):
        load_values(r, r).start()

    def quarter_of(q):
        return pl.ds(pl.multiple_of(q * quarter, quarter), quarter)

    pl.semaphore_wait(barrier, 31)

    half_deep = deep // 2

    def x_copy(i, block, part, device):
        rows = proj_rows(block, part * half_deep, half_deep)
        src = refs.attn_out_w.at[pl.ds(part * half_deep, half_deep)] if i < 4 else s.v_proj.at[0, rows]
        return remote(src, s.v_proj.at[0, rows], s.x_send.at[i], s.x_recv.at[i], device)

    along = [
        x_copy(0, x, 0, right),
        x_copy(1, x, 1, left),
        x_copy(2, x, 1, right),
        x_copy(3, x, 0, left),
    ]
    to_core = [
        remote(
            refs.attn_out_w, s.v_proj.at[1, proj_rows(x)], s.core_send.at[0], s.core_recv.at[0], core
        )
    ]
    for i, (src, dst) in enumerate(
        [(refs.w_gate, s.v_gate), (refs.w_up, s.v_up), (refs.w_down, s.v_down)]
    ):
        to_core.append(
            remote(src.at[0], dst.at[1], s.core_send.at[i + 1], s.core_recv.at[i + 1], core)
        )
    early = [
        remote(s.info.at[0], s.info.at[2], s.early_send.at[0], s.early_recv.at[0], beside),
        remote(s.info.at[0], s.info.at[1], s.early_send.at[1], s.early_recv.at[1], across),
        remote(s.info.at[0], s.info.at[3], s.early_send.at[2], s.early_recv.at[2], diagonal),
        remote(s.hid_out, s.hid_in, s.early_send.at[3], s.early_recv.at[3], beside),
    ]
    for copy in along[:2] + to_core[:1]:
        copy.start()

    for copy in small:
        copy.wait()
    for h in range(s.in_query.shape[1] // HD):
        s.q_rows[:, h, :] = s.in_query[:, h * HD : (h + 1) * HD].astype(f32)
    for g in range(s.in_key_new.shape[1] // HD):
        s.k_new[:, g, :] = s.in_key_new[:, g * HD : (g + 1) * HD].astype(f32)
        s.v_new[:, g, :] = s.in_value_new[:, g * HD : (g + 1) * HD].astype(f32)

    square = (ROWS, ROWS)
    row_of = lax.broadcasted_iota(jnp.int32, square, 0)
    column_of = lax.broadcasted_iota(jnp.int32, square, 1)
    unit_matrix = jnp.where(row_of == column_of, 1.0, 0.0).astype(bf16)

    def turned(value):
        return lax.dot_general(
            unit_matrix, value, (((1,), (1,)), ((), ())), preferred_element_type=f32
        )

    routes = turned(s.in_routes[...].astype(f32).astype(bf16)).astype(jnp.int32)
    rest = s.in_gate_weights[...]
    gate_weights = jnp.zeros((ROWS, TOP), f32)
    for _ in range(3):
        piece = rest.astype(bf16)
        gate_weights = gate_weights + turned(piece)
        rest = rest - piece.astype(f32)
    lane = lax.broadcasted_iota(jnp.int32, (ROWS, 128), 1)
    named = jnp.zeros((ROWS, 128), f32)
    weight = jnp.zeros((ROWS, 128), f32)
    for k in range(TOP):
        hit = routes[:, k : k + 1] == lane % EXPERTS
        named = named + jnp.where(hit, 1.0, 0.0)
        weight = weight + jnp.where(hit, gate_weights[:, k : k + 1], 0.0)
    rank = jnp.dot(
        jnp.where(column_of < row_of, 1.0, 0.0).astype(bf16), named.astype(bf16), preferred_element_type=f32
    )
    high = weight.astype(bf16).astype(f32)
    middle = (weight - high).astype(bf16).astype(f32)
    kind = lane // EXPERTS
    s.info[0] = jnp.where(
        kind == 0,
        jnp.where(named > 0.0, rank, -1.0),
        jnp.where(kind == 1, high, jnp.where(kind == 2, middle, weight - high - middle)),
    )

    s.hid_out[:, :quarter] = s.in_hidden_in[:, quarter_of(other_replica)]
    s.hid_out[:, quarter:] = s.in_hidden_in[:, quarter_of(other_sibling)]
    s.mid[:16, :quarter] = s.in_hidden_in[:, quarter_of(replica)].astype(f32)
    s.mid[:16, quarter:] = s.in_hidden_in[:, quarter_of(sibling)].astype(f32)
    s.gain[:, :quarter] = s.in_norm_gain[:, quarter_of(replica)]
    s.gain[:, quarter:] = s.in_norm_gain[:, quarter_of(sibling)]
    for copy in early + to_core[1:2]:
        copy.start()

    for b in range(n_rows // RING):
        last_turn = b == n_rows // RING - 1

        @pl.loop(0, RING, unroll=2)
        def _(i):
            load_keys(b * RING + i, i).wait()
            scores_row(s, b * RING + i, i)

        if b == 0:
            for copy in along[2:]:
                copy.start()
        if not last_turn:
            for i in range(RING):
                load_keys((b + 1) * RING + i, i).start()

        @pl.loop(0, RING, unroll=2)
        def _(i):
            softmax_row(refs, s, b * RING + i, i)

        @pl.loop(0, RING, unroll=2)
        def _(i):
            load_values(b * RING + i, i).wait()
            values_row(s, b * RING + i, i)

        if not last_turn:
            for i in range(RING):
                load_values((b + 1) * RING + i, i).start()
        if b == 0:
            along[0].wait_recv()
            along[1].wait_recv()
            onward = [
                x_copy(4, (x + 3) % 4, 0, right),
                x_copy(5, (x + 1) % 4, 1, left),
            ]
            for copy in onward + to_core[2:3]:
                copy.start()


    for h in range(s.o_rows.shape[1]):
        s.attn[h // 8, :, h % 8 * HD : (h % 8 + 1) * HD] = s.o_rows[:, h, :].astype(bf16)

    def heads_copy(h, t):
        there = group_shifted(expert, t, 1)
        return remote(
            s.attn.at[there // 4],
            s.heads.at[h, t],
            s.heads_send.at[h, t],
            s.heads_recv.at[h, t],
            (other_replica if h else replica, there),
        )

    for h in (1, 0):

        @pl.loop(1 - h, 8)
        def _(t):
            heads_copy(h, t).start()

    s.heads[0, 0] = s.attn[expert // 4]

    for copy in along[2:]:
        copy.wait_recv()
    for copy in onward:
        copy.wait_recv()
    for i, step in enumerate((1, 3, 2)):
        rows = proj_rows((x + step) % 4)
        to_core.append(
            remote(
                s.v_proj.at[0, rows],
                s.v_proj.at[1, rows],
                s.core_send.at[i + 4],
                s.core_recv.at[i + 4],
                core,
            )
        )
        to_core[-1].start()

    for load in loads[1:]:
        load.start()

    for copy in early:
        copy.wait_recv()
    s.mid[16:, :] = s.hid_in[...].astype(f32)
    slot = lax.broadcasted_iota(jnp.int32, (128, 256), 1)
    step = slot // 16
    dz = step % 8 // 2
    dx = 2 * (step % 2) + (dz + step // 8) % 2
    taker = plane * 16 + (z + dz) % 4 * 4 + (x + dx) % 4
    entry = lax.broadcasted_iota(jnp.int32, (128, 256), 0)
    slot32 = lax.broadcasted_iota(jnp.int32, (32, 256), 1)
    row32 = lax.broadcasted_iota(jnp.int32, (32, 256), 0)
    for h in range(2):
        infos = s.info[2 * h : 2 * h + 2].reshape(32, 128).astype(bf16)
        picked = [
            jnp.dot(
                infos,
                jnp.where(entry == taker + EXPERTS * i, 1.0, 0.0).astype(bf16),
                preferred_element_type=f32,
            )
            for i in range(4)
        ]
        hit = (picked[0] == (slot32 % CAP).astype(f32)) & (slot32 // CAP % 2 == row32 // ROWS)
        s.placing[h] = jnp.where(hit, 1.0, 0.0).astype(bf16)
        for i in range(3):
            s.weighting[h, 32 * i : 32 * i + 32, :] = jnp.where(hit, picked[i + 1], 0.0).astype(bf16)

    def sums_copy(h, t):
        return remote(
            s.sums.at[h, t],
            s.sums_in.at[h, t],
            s.sums_send.at[h, t],
            s.sums_recv.at[h, t],
            (replica, group_shifted(expert, t, -1)),
        )

    loads[0].wait()
    to_core[0].wait_recv()
    for copy in to_core[4:]:
        copy.wait_recv()
    to_core[3].start()
    for h in (1, 0):

        @pl.loop(1 - h, 8)
        def _(t):
            heads_copy(h, t).wait_recv()

        for q in range(2):

            @pl.loop(0, quarter // TILE)
            def _(n):
                value = jnp.dot(
                    s.heads[h].reshape(8 * ROWS, quarter),
                    s.v_proj[q, :, columns(n)],
                    preferred_element_type=f32,
                )
                at = pl.multiple_of(q * quarter + n * TILE, TILE)
                s.sums[h, :, :, pl.ds(at, TILE)] = value.astype(bf16).reshape(8, ROWS, TILE)

        @pl.loop(1, 8)
        def _(t):
            sums_copy(h, t).start()

    over = [
        remote(
            s.rows_all.at[h, pl.ds(0, ROWS)],
            s.rows_all.at[h, pl.ds(ROWS, ROWS)],
            s.over_send.at[h],
            s.over_recv.at[h],
            across,
        )
        for h in range(2)
    ]

    def finish_rows(h):
        @pl.loop(1, 8)
        def _(t):
            sums_copy(h, t).wait_recv()

        rows = pl.ds(ROWS * h, ROWS)

        @pl.loop(0, half // TILE)
        def _(n):
            total = s.mid[rows, columns(n)] + s.sums[h, 0, :, columns(n)].astype(f32)
            for t in range(1, 8):
                total = total + s.sums_in[h, t, :, columns(n)].astype(f32)
            s.mid[rows, columns(n)] = total
            s.rows_all[h, :ROWS, columns(n)] = (total * s.gain[:, columns(n)]).astype(bf16)

        over[h].start()
        mid = s.mid[rows, :]
        s.square_out[rows, :] = jnp.broadcast_to(
            jnp.sum(mid * mid, axis=-1, keepdims=True), (ROWS, 128)
        )

    def dispatch(h, i):
        rows = pl.ds(pl.multiple_of(i * 16, 16), 16)
        return remote(
            s.outgoing.at[h, rows],
            s.block.at[h, rows],
            s.disp_send.at[h, i],
            s.disp_recv.at[h, i],
            (replica, shifted(expert, i, 1)),
        )

    def send_rows(h, c):
        if c == 0:
            over[h].wait_recv()
        first, number = CHUNKS[c]
        slots = pl.ds(16 * first, 16 * number)

        @pl.loop(0, half // TILE)
        def _(n):
            s.outgoing[h, slots, columns(n)] = lax.dot_general(
                s.placing[h, :, slots],
                s.rows_all[h, :, columns(n)],
                (((0,), (0,)), ((), ())),
                preferred_element_type=f32,
            ).astype(bf16)

        @pl.loop(max(1, first), first + number)
        def _(i):
            dispatch(h, i).start()

        if first == 0:
            s.block[h, :16, :] = s.outgoing[h, :16, :]

    finish_rows(1)
    send_rows(1, 0)
    finish_rows(0)
    squares = [
        remote(
            s.square_out, s.square_in.at[i], s.square_send.at[i], s.square_recv.at[i], device
        )
        for i, device in enumerate((beside, across, diagonal))
    ]
    for copy in squares:
        copy.start()
    send_rows(1, 1)
    send_rows(0, 0)

    def scale_copy(i):
        slots = pl.ds(pl.multiple_of(i * 16, 16), 16)
        return remote(
            s.scale_out.at[slots],
            s.scale_in.at[slots],
            s.scale_send.at[i],
            s.scale_recv.at[i],
            (replica, shifted(expert, i, 1)),
        )

    def send_scales():
        for copy in squares:
            copy.wait_recv()
        total = jnp.concatenate(
            [
                s.square_out[:ROWS, :] + s.square_in[0, ROWS:, :],
                s.square_in[1, :ROWS, :] + s.square_in[2, ROWS:, :],
            ],
            axis=0,
        )
        rest = lax.rsqrt(total / (2.0 * half) + 1e-06)
        value = jnp.zeros((256, 128), f32)
        for _ in range(3):
            piece = rest.astype(bf16)
            value = value + lax.dot_general(
                s.placing[0], piece, (((0,), (0,)), ((), ())), preferred_element_type=f32
            )
            rest = rest - piece.astype(f32)
        s.scale_out[...] = value

        @pl.loop(1, 16)
        def _(i):
            scale_copy(i).start()

        s.scale_in[:16, :] = value[:16]

    tiles = hidden // TILE

    def slots_of(c, chunks=CHUNKS):
        first, number = chunks[c]
        return pl.ds(16 * first, 16 * number)

    def gate_up(h, c, n):
        for which, mats in enumerate((s.v_gate, s.v_up)):
            yield which, jnp.dot(
                s.block[h, slots_of(c), :quarter],
                mats[0, :, columns(n)],
                preferred_element_type=f32,
            ) + jnp.dot(
                s.block[h, slots_of(c), quarter:],
                mats[1, :, columns(n)],
                preferred_element_type=f32,
            )

    def part_copy(c, n):
        return remote(
            s.part_out.at[n, :, slots_of(c)],
            s.part_in.at[n, :, slots_of(c)],
            s.part_send.at[c, n],
            s.part_recv.at[c, n],
            beside,
        )

    def wait_rows(h, c):
        first, number = CHUNKS[c]

        @pl.loop(max(1, first), first + number)
        def _(i):
            dispatch(h, i).wait_recv()

    loads[1].wait()
    loads[2].wait()
    to_core[1].wait_recv()
    to_core[2].wait_recv()
    for c in range(len(CHUNKS)):
        wait_rows(1, c)

        @pl.loop(0, tiles)
        def _(n):
            for which, value in gate_up(1, c, n):
                s.part_out[n, which, slots_of(c), :] = value.astype(bf16)
            part_copy(c, n).start()

        if c == 0:
            send_rows(0, 1)
            send_scales()

    def own_part(c):
        wait_rows(0, c)

        @pl.loop(0, tiles)
        def _(n):
            for which, value in gate_up(0, c, n):
                s.part_own[n, which, slots_of(c), :] = value

    def give_back(h, i):
        rows = pl.ds(pl.multiple_of(i * 16, 16), 16)
        return remote(
            s.result.at[h, rows],
            s.returned.at[h, rows],
            s.ret_send.at[h, i],
            s.ret_recv.at[h, i],
            (replica, shifted(expert, i, -1)),
        )

    def down(h, c, chunks):
        first, number = chunks[c]
        for q in range(2):

            @pl.loop(0, quarter // TILE)
            def _(n):
                value = jnp.zeros((16 * number, TILE), f32)
                for k in range(tiles):
                    value = value + jnp.dot(
                        s.units[h, k, slots_of(c, chunks), :],
                        s.v_down[q, k * TILE : (k + 1) * TILE, columns(n)],
                        preferred_element_type=f32,
                    )
                at = pl.multiple_of(q * quarter + n * TILE, TILE)
                s.result[h, slots_of(c, chunks), pl.ds(at, TILE)] = value.astype(bf16)

        @pl.loop(max(1, first), first + number)
        def _(i):
            give_back(h, i).start()

        if first == 0:
            s.returned[h, :16, :] = s.result[h, :16, :]

    def unit_copy(c, n):
        return remote(
            s.units.at[0, n, slots_of(c, SHARES)],
            s.units.at[1, n, slots_of(c, SHARES)],
            s.unit_send.at[c, n],
            s.unit_recv.at[c, n],
            beside,
        )

    def combine(h, begin, end):
        @pl.loop(max(1, begin), end)
        def _(i):
            give_back(h, i).wait_recv()

        slots = pl.ds(16 * begin, 16 * (end - begin))

        @pl.loop(0, half // TILE)
        def _(n):
            three = jnp.dot(
                s.weighting[h, :, slots],
                s.returned[h, slots, columns(n)],
                preferred_element_type=f32,
            )
            value = three[:32] + three[32:64] + three[64:]
            s.mixed[h, :, columns(n)] = value if begin == 0 else s.mixed[h, :, columns(n)] + value

    @pl.loop(1, 16)
    def _(i):
        scale_copy(i).wait_recv()

    own_part(0)
    for c in range(len(CHUNKS)):

        @pl.loop(0, tiles)
        def _(n):
            part_copy(c, n).wait_recv()
            scale = s.scale_in[slots_of(c), :1]
            gate = s.part_own[n, 0, slots_of(c), :] + s.part_in[n, 0, slots_of(c), :].astype(f32)
            up_val = s.part_own[n, 1, slots_of(c), :] + s.part_in[n, 1, slots_of(c), :].astype(f32)
            gate, up_val = gate * scale, up_val * scale
            s.units[0, n, slots_of(c), :] = (gate / (1.0 + jnp.exp(-gate)) * up_val).astype(bf16)
            unit_copy(c, n).start()

        if c == 1:

            @pl.loop(0, tiles)
            def _(n):
                unit_copy(2, n).start()

        if c == 0:
            loads[3].wait()
            to_core[3].wait_recv()
        if c + 1 < len(CHUNKS):
            own_part(c + 1)
        down(0, c, CHUNKS)
    last = [
        remote(s.last_out.at[i], s.last_in.at[i], s.last_send.at[i], s.last_recv.at[i], device)
        for i, device in enumerate((across, beside, diagonal))
    ]
    for c in range(len(SHARES)):

        @pl.loop(0, tiles)
        def _(n):
            unit_copy(c, n).wait_recv()

        down(1, c, SHARES)
        if c == 1:
            combine(0, 0, 16)
            s.last_out[0] = s.mixed[0, 16:, :].astype(bf16)
            last[0].start()
    for copy in along + early + to_core + onward + over + squares:
        copy.wait_send()

    @pl.loop(1, 8)
    def _(i):
        heads_copy(0, i).wait_send()
        heads_copy(1, i).wait_send()
        sums_copy(0, i).wait_send()
        sums_copy(1, i).wait_send()
        give_back(1, i).wait_send()

    heads_copy(1, 0).wait_send()

    @pl.loop(1, 16)
    def _(i):
        dispatch(0, i).wait_send()
        dispatch(1, i).wait_send()
        scale_copy(i).wait_send()
        give_back(0, i).wait_send()

    @pl.loop(0, tiles)
    def _(n):
        part_copy(0, n).wait_send()
        part_copy(1, n).wait_send()
        unit_copy(0, n).wait_send()

    combine(1, 0, 8)
    combine(1, 8, 12)
    combine(1, 12, 16)
    s.last_out[1] = (s.mid[16:, :] + s.mixed[1, :16, :]).astype(bf16)
    s.last_out[2] = s.mixed[1, 16:, :].astype(bf16)
    last[1].start()
    last[2].start()
    for copy in last:
        copy.wait_recv()
    here = s.mid[:16, :] + s.mixed[0, :16, :]
    refs.near_sum[:, quarter_of(replica)] = here[:, :quarter]
    refs.near_sum[:, quarter_of(sibling)] = here[:, quarter:]
    there = s.last_in[1].astype(f32)
    refs.near_sum[:, quarter_of(other_replica)] = there[:, :quarter]
    refs.near_sum[:, quarter_of(other_sibling)] = there[:, quarter:]
    refs.far_sum[:, quarter_of(replica)] = s.last_in[0, :, :quarter]
    refs.far_sum[:, quarter_of(sibling)] = s.last_in[0, :, quarter:]
    refs.far_sum[:, quarter_of(other_replica)] = s.last_in[2, :, :quarter]
    refs.far_sum[:, quarter_of(other_sibling)] = s.last_in[2, :, quarter:]

    for copy in last:
        copy.wait_send()

    @pl.loop(8, 16)
    def _(i):
        give_back(1, i).wait_send()

    @pl.loop(0, tiles)
    def _(n):
        unit_copy(1, n).wait_send()
        unit_copy(2, n).wait_send()


ARGS = (
    "hidden_in",
    "query",
    "key_new",
    "value_new",
    "key_cache",
    "value_cache",
    "cache_len",
    "attn_out_w",
    "norm_gain",
    "routes",
    "gate_weights",
    "w_gate",
    "w_up",
    "w_down",
)


SMALL = (
    "query",
    "key_new",
    "value_new",
    "routes",
    "gate_weights",
    "hidden_in",
    "norm_gain",
)


def body(*args):
    f32, bf16 = jnp.float32, jnp.bfloat16
    given = dict(zip(ARGS, args))
    given["norm_gain"] = given["norm_gain"][None, :]
    given["routes"], given["gate_weights"] = given["routes"].T, given["gate_weights"].T
    n_rows, width = given["hidden_in"].shape
    groups, context, head_size = given["key_cache"].shape[1:]
    heads = given["query"].shape[1] // head_size
    _, quarter, hidden = given["w_gate"].shape
    deep = given["attn_out_w"].shape[0]
    half, tiles = 2 * quarter, hidden // TILE
    vmem, anywhere = pl.BlockSpec(memory_space=pltpu.VMEM), pl.BlockSpec(memory_space=pl.ANY)
    places = {name: anywhere for name in ARGS}
    places["cache_len"] = pl.BlockSpec(memory_space=pltpu.SMEM)
    scratch = {"in_" + name: (given[name].shape, given[name].dtype) for name in SMALL}
    scratch |= dict(
        k_ring=((RING, groups, context, head_size), bf16),
        v_ring=((RING, groups, context, head_size), bf16),
        q_rows=((n_rows, heads, head_size), f32),
        o_rows=((n_rows, heads, head_size), f32),
        scores=((RING, heads, context), f32),
        probs=((RING, heads, context), bf16),
        own_part=((RING, heads, head_size), f32),
        k_new=((n_rows, groups, head_size), f32),
        v_new=((n_rows, groups, head_size), f32),
        info=((4, ROWS, 128), f32),
        hid_out=((ROWS, half), bf16),
        hid_in=((ROWS, half), bf16),
        mid=((32, half), f32),
        gain=((1, half), f32),
        v_proj=((2, 4 * deep, quarter), bf16),
        v_gate=((2, quarter, hidden), bf16),
        v_up=((2, quarter, hidden), bf16),
        v_down=((2, hidden, quarter), bf16),
        attn=((8, ROWS, quarter), bf16),
        heads=((2, 8, ROWS, quarter), bf16),
        sums=((2, 8, ROWS, half), bf16),
        sums_in=((2, 8, ROWS, half), bf16),
        placing=((2, 32, 256), bf16),
        weighting=((2, 96, 256), bf16),
        square_out=((32, 128), f32),
        square_in=((3, 32, 128), f32),
        scale_out=((256, 128), f32),
        scale_in=((256, 128), f32),
        rows_all=((2, 32, half), bf16),
        outgoing=((2, 256, half), bf16),
        block=((2, 256, half), bf16),
        part_out=((tiles, 2, 256, TILE), bf16),
        part_in=((tiles, 2, 256, TILE), bf16),
        part_own=((tiles, 2, 256, TILE), f32),
        units=((2, tiles, 256, TILE), bf16),
        result=((2, 256, half), bf16),
        returned=((2, 256, half), bf16),
        mixed=((2, 32, half), f32),
        last_out=((3, 16, half), bf16),
        last_in=((3, 16, half), bf16),
    )
    semaphores = dict(
        k_sem=(RING,),
        v_sem=(RING,),
        load_sem=(4,),
        small_sem=(len(SMALL),),
        x_send=(6,),
        x_recv=(6,),
        core_send=(7,),
        core_recv=(7,),
        early_send=(4,),
        early_recv=(4,),
        heads_send=(2, 8),
        heads_recv=(2, 8),
        sums_send=(2, 8),
        sums_recv=(2, 8),
        over_send=(2,),
        over_recv=(2,),
        square_send=(3,),
        square_recv=(3,),
        scale_send=(16,),
        scale_recv=(16,),
        disp_send=(2, 16),
        disp_recv=(2, 16),
        part_send=(len(CHUNKS), tiles),
        part_recv=(len(CHUNKS), tiles),
        unit_send=(len(SHARES), tiles),
        unit_recv=(len(SHARES), tiles),
        ret_send=(2, 16),
        ret_recv=(2, 16),
        last_send=(3,),
        last_recv=(3,),
    )
    names = ARGS + ("near_sum", "far_sum")
    scratch_names = list(scratch) + list(semaphores)

    def kernel(*all_refs):
        layer_kernel(names, scratch_names, *all_refs)

    near_sum, far_sum = pl.pallas_call(
        kernel,
        out_shape=(
            jax.ShapeDtypeStruct((n_rows, width), f32),
            jax.ShapeDtypeStruct((n_rows, width), bf16),
        ),
        in_specs=[places[name] for name in ARGS],
        out_specs=(vmem, vmem),
        scratch_shapes=[pltpu.VMEM(*v) for v in scratch.values()]
        + [pltpu.SemaphoreType.DMA(v) for v in semaphores.values()],
        compiler_params=pltpu.CompilerParams(
            collective_id=0, has_side_effects=True, vmem_limit_bytes=60 * 1024 * 1024
        ),
        cost_estimate=pl.CostEstimate(
            flops=12 * 10**9, bytes_accessed=40 * 10**6, transcendentals=10**6
        ),
    )(*given.values())
    return (near_sum + far_sum.astype(f32)).astype(bf16)


def solution(mesh):
    placed = (
        P(("replica", "expert"), None),
        P(("replica", "expert"), None),
        P(("replica", "expert"), None),
        P(("replica", "expert"), None),
        P(("replica", "expert"), None, None, None),
        P(("replica", "expert"), None, None, None),
        P(("replica", "expert")),
        P("expert", "replica"),
        P(),
        P(("replica", "expert"), None),
        P(("replica", "expert"), None),
        P("expert", "replica", None),
        P("expert", "replica", None),
        P("expert", None, "replica"),
    )
    return jax.shard_map(
        body, mesh=mesh, in_specs=placed, out_specs=P(("replica", "expert"), None), check_vma=False
    )
```

```python
import types

import jax
import jax.numpy as jnp
from jax import lax
from jax.experimental import pallas as pl
from jax.experimental.pallas import tpu as pltpu
from jax.sharding import PartitionSpec as P

HD = 128
TOP = 8
EXPERTS = 32
CAP = 8
ROWS = 16
RING = 8
TILE = 512
CHUNKS = ((0, 8), (8, 8))
SHARES = ((0, 8), (8, 4), (12, 4))
MESH = pl.DeviceIdType.MESH


def offset(s):
    dz = s % 8 // 2
    return dz, 2 * (s % 2) + (dz + s // 8) % 2


def shifted(expert, s, sign):
    dz, dx = offset(s)
    plane, z, x = expert // 16, expert // 4 % 4, expert % 4
    return plane * 16 + (z + 4 + sign * dz) % 4 * 4 + (x + 4 + sign * dx) % 4


def group_shifted(expert, t, sign):
    plane, z, x = expert // 16, expert // 4 % 4, expert % 4
    return (plane + t // 4) % 2 * 16 + (z + 4 + sign * (t % 4)) % 4 * 4 + x


def remote(src, dst, send, recv, device):
    return pltpu.make_async_remote_copy(
        src_ref=src,
        dst_ref=dst,
        send_sem=send,
        recv_sem=recv,
        device_id=device,
        device_id_type=MESH,
    )


def columns(n):
    return pl.ds(pl.multiple_of(n * TILE, TILE), TILE)


def scores_row(s, r, slot):
    groups = s.k_ring.shape[1]
    heads = s.q_rows.shape[1] // groups
    for g in range(groups):
        mine = pl.ds(g * heads, heads)
        s.scores[slot, mine, :] = lax.dot_general(
            s.q_rows[r, mine, :].astype(jnp.bfloat16),
            s.k_ring[slot, g],
            (((1,), (1,)), ((), ())),
            preferred_element_type=jnp.float32,
        )


def softmax_row(refs, s, r, slot):
    f32, bf16 = jnp.float32, jnp.bfloat16
    groups = s.k_ring.shape[1]
    heads = s.q_rows.shape[1] // groups
    scale = HD ** (-0.5)
    live = lax.broadcasted_iota(jnp.int32, s.scores.shape[1:], 1) < refs.cache_len[r]
    cached = jnp.where(live, s.scores[slot] * scale, -jnp.inf)
    own = [
        jnp.sum(
            s.q_rows[r, g * heads : (g + 1) * heads, :] * s.k_new[r, g : g + 1, :],
            axis=-1,
            keepdims=True,
        )
        for g in range(groups)
    ]
    own = jnp.concatenate(own, axis=0) * scale
    highest = jnp.maximum(jnp.max(cached, axis=-1, keepdims=True), own)
    cached_exp = jnp.exp(cached - highest)
    own_exp = jnp.exp(own - highest)
    inverse = 1.0 / (jnp.sum(cached_exp, axis=-1, keepdims=True) + own_exp)
    s.probs[slot] = (cached_exp * inverse).astype(bf16)
    own_prob = (own_exp * inverse).astype(bf16).astype(f32)
    for g in range(groups):
        mine = pl.ds(g * heads, heads)
        s.own_part[slot, mine, :] = (
            own_prob[g * heads : (g + 1) * heads] * s.v_new[r, g : g + 1, :]
        )


def values_row(s, r, slot):
    groups = s.k_ring.shape[1]
    heads = s.q_rows.shape[1] // groups
    for g in range(groups):
        mine = pl.ds(g * heads, heads)
        mixed = jnp.dot(
            s.probs[slot, mine, :], s.v_ring[slot, g], preferred_element_type=jnp.float32
        )
        s.o_rows[r, mine, :] = mixed + s.own_part[slot, mine, :]


def layer_kernel(names, scratch_names, *all_refs):
    refs = types.SimpleNamespace(**dict(zip(names, all_refs)))
    s = types.SimpleNamespace(**dict(zip(scratch_names, all_refs[len(names) :])))
    f32, bf16 = jnp.float32, jnp.bfloat16
    replica, expert = lax.axis_index("replica"), lax.axis_index("expert")
    plane, z, x = expert // 16, expert // 4 % 4, expert % 4
    sibling = replica // 2 * 2 + (replica + 1) % 2
    other_replica, other_plane = (replica + 2) % 4, (expert + 16) % 32
    other_sibling = other_replica // 2 * 2 + (other_replica + 1) % 2
    beside, across = (other_replica, expert), (replica, other_plane)
    diagonal, core = (other_replica, other_plane), (sibling, expert)
    line = expert // 4 * 4
    right, left = (replica, line + (x + 1) % 4), (replica, line + (x + 3) % 4)
    hidden, quarter = s.v_gate.shape[2], s.v_gate.shape[1]
    half = 2 * quarter
    n_rows = refs.cache_len.shape[0]
    deep = refs.attn_out_w.shape[0]

    barrier = pltpu.get_barrier_semaphore()

    def greet(device):
        pl.semaphore_signal(barrier, inc=1, device_id=device, device_id_type=MESH)

    @pl.loop(1, 16)
    def _(i):
        greet((replica, shifted(expert, i, 1)))

    @pl.loop(1, 8)
    def _(t):
        greet((replica, group_shifted(expert, t, 1)))

    @pl.loop(0, 8)
    def _(t):
        greet((other_replica, group_shifted(expert, t, 1)))

    greet(core)

    small = [
        pltpu.make_async_copy(getattr(refs, name), getattr(s, "in_" + name), s.small_sem.at[i])
        for i, name in enumerate(SMALL)
    ]
    for copy in small:
        copy.start()

    def load_keys(r, slot):
        return pltpu.make_async_copy(refs.key_cache.at[r], s.k_ring.at[slot], s.k_sem.at[slot])

    def load_values(r, slot):
        return pltpu.make_async_copy(refs.value_cache.at[r], s.v_ring.at[slot], s.v_sem.at[slot])

    def proj_rows(block, start=0, count=deep):
        return pl.ds(pl.multiple_of(block * deep + start, 16), count)

    loads = [
        pltpu.make_async_copy(src, dst, s.load_sem.at[i])
        for i, (src, dst) in enumerate(
            [
                (refs.attn_out_w, s.v_proj.at[0, proj_rows(x)]),
                (refs.w_gate.at[0], s.v_gate.at[0]),
                (refs.w_up.at[0], s.v_up.at[0]),
                (refs.w_down.at[0], s.v_down.at[0]),
            ]
        )
    ]
    for r in range(RING):
        load_keys(r, r).start()
    loads[0].start()
    for r in range(RING):
        load_values(r, r).start()

    def quarter_of(q):
        return pl.ds(pl.multiple_of(q * quarter, quarter), quarter)

    pl.semaphore_wait(barrier, 31)

    half_deep = deep // 2

    def x_copy(i, block, part, device):
        rows = proj_rows(block, part * half_deep, half_deep)
        src = refs.attn_out_w.at[pl.ds(part * half_deep, half_deep)] if i < 4 else s.v_proj.at[0, rows]
        return remote(src, s.v_proj.at[0, rows], s.x_send.at[i], s.x_recv.at[i], device)

    along = [
        x_copy(0, x, 0, right),
        x_copy(1, x, 1, left),
        x_copy(2, x, 1, right),
        x_copy(3, x, 0, left),
    ]
    to_core = [
        remote(
            refs.attn_out_w, s.v_proj.at[1, proj_rows(x)], s.core_send.at[0], s.core_recv.at[0], core
        )
    ]
    for i, (src, dst) in enumerate(
        [(refs.w_gate, s.v_gate), (refs.w_up, s.v_up), (refs.w_down, s.v_down)]
    ):
        to_core.append(
            remote(src.at[0], dst.at[1], s.core_send.at[i + 1], s.core_recv.at[i + 1], core)
        )
    early = [
        remote(s.info.at[0], s.info.at[2], s.early_send.at[0], s.early_recv.at[0], beside),
        remote(s.info.at[0], s.info.at[1], s.early_send.at[1], s.early_recv.at[1], across),
        remote(s.info.at[0], s.info.at[3], s.early_send.at[2], s.early_recv.at[2], diagonal),
        remote(s.hid_out, s.hid_in, s.early_send.at[3], s.early_recv.at[3], beside),
    ]
    for copy in along[:2] + to_core[:1]:
        copy.start()

    for copy in small:
        copy.wait()
    for h in range(s.in_query.shape[1] // HD):
        s.q_rows[:, h, :] = s.in_query[:, h * HD : (h + 1) * HD].astype(f32)
    for g in range(s.in_key_new.shape[1] // HD):
        s.k_new[:, g, :] = s.in_key_new[:, g * HD : (g + 1) * HD].astype(f32)
        s.v_new[:, g, :] = s.in_value_new[:, g * HD : (g + 1) * HD].astype(f32)

    square = (ROWS, ROWS)
    row_of = lax.broadcasted_iota(jnp.int32, square, 0)
    column_of = lax.broadcasted_iota(jnp.int32, square, 1)
    unit_matrix = jnp.where(row_of == column_of, 1.0, 0.0).astype(bf16)

    def turned(value):
        return lax.dot_general(
            unit_matrix, value, (((1,), (1,)), ((), ())), preferred_element_type=f32
        )

    routes = turned(s.in_routes[...].astype(f32).astype(bf16)).astype(jnp.int32)
    rest = s.in_gate_weights[...]
    gate_weights = jnp.zeros((ROWS, TOP), f32)
    for _ in range(3):
        piece = rest.astype(bf16)
        gate_weights = gate_weights + turned(piece)
        rest = rest - piece.astype(f32)
    lane = lax.broadcasted_iota(jnp.int32, (ROWS, 128), 1)
    named = jnp.zeros((ROWS, 128), f32)
    weight = jnp.zeros((ROWS, 128), f32)
    for k in range(TOP):
        hit = routes[:, k : k + 1] == lane % EXPERTS
        named = named + jnp.where(hit, 1.0, 0.0)
        weight = weight + jnp.where(hit, gate_weights[:, k : k + 1], 0.0)
    rank = jnp.dot(
        jnp.where(column_of < row_of, 1.0, 0.0).astype(bf16), named.astype(bf16), preferred_element_type=f32
    )
    high = weight.astype(bf16).astype(f32)
    middle = (weight - high).astype(bf16).astype(f32)
    kind = lane // EXPERTS
    s.info[0] = jnp.where(
        kind == 0,
        jnp.where(named > 0.0, rank, -1.0),
        jnp.where(kind == 1, high, jnp.where(kind == 2, middle, weight - high - middle)),
    )

    s.hid_out[:, :quarter] = s.in_hidden_in[:, quarter_of(other_replica)]
    s.hid_out[:, quarter:] = s.in_hidden_in[:, quarter_of(other_sibling)]
    s.mid[:16, :quarter] = s.in_hidden_in[:, quarter_of(replica)].astype(f32)
    s.mid[:16, quarter:] = s.in_hidden_in[:, quarter_of(sibling)].astype(f32)
    s.gain[:, :quarter] = s.in_norm_gain[:, quarter_of(replica)]
    s.gain[:, quarter:] = s.in_norm_gain[:, quarter_of(sibling)]
    for copy in early + to_core[1:2]:
        copy.start()

    for b in range(n_rows // RING):
        last_turn = b == n_rows // RING - 1

        @pl.loop(0, RING, unroll=2)
        def _(i):
            load_keys(b * RING + i, i).wait()
            scores_row(s, b * RING + i, i)

        if b == 0:
            for copy in along[2:]:
                copy.start()
        if not last_turn:
            for i in range(RING):
                load_keys((b + 1) * RING + i, i).start()

        @pl.loop(0, RING, unroll=2)
        def _(i):
            softmax_row(refs, s, b * RING + i, i)

        @pl.loop(0, RING, unroll=2)
        def _(i):
            load_values(b * RING + i, i).wait()
            values_row(s, b * RING + i, i)

        if not last_turn:
            for i in range(RING):
                load_values((b + 1) * RING + i, i).start()
        if b == 0:
            along[0].wait_recv()
            along[1].wait_recv()
            onward = [
                x_copy(4, (x + 3) % 4, 0, right),
                x_copy(5, (x + 1) % 4, 1, left),
            ]
            for copy in onward + to_core[2:3]:
                copy.start()


    for h in range(s.o_rows.shape[1]):
        s.attn[h // 8, :, h % 8 * HD : (h % 8 + 1) * HD] = s.o_rows[:, h, :].astype(bf16)

    def heads_copy(h, t):
        there = group_shifted(expert, t, 1)
        return remote(
            s.attn.at[there // 4],
            s.heads.at[h, t],
            s.heads_send.at[h, t],
            s.heads_recv.at[h, t],
            (other_replica if h else replica, there),
        )

    for h in (1, 0):

        @pl.loop(1 - h, 8)
        def _(t):
            heads_copy(h, t).start()

    s.heads[0, 0] = s.attn[expert // 4]

    for copy in along[2:]:
        copy.wait_recv()
    for copy in onward:
        copy.wait_recv()
    for i, step in enumerate((1, 3, 2)):
        rows = proj_rows((x + step) % 4)
        to_core.append(
            remote(
                s.v_proj.at[0, rows],
                s.v_proj.at[1, rows],
                s.core_send.at[i + 4],
                s.core_recv.at[i + 4],
                core,
            )
        )
        to_core[-1].start()

    for load in loads[1:]:
        load.start()

    for copy in early:
        copy.wait_recv()
    s.mid[16:, :] = s.hid_in[...].astype(f32)
    slot = lax.broadcasted_iota(jnp.int32, (128, 256), 1)
    step = slot // 16
    dz = step % 8 // 2
    dx = 2 * (step % 2) + (dz + step // 8) % 2
    taker = plane * 16 + (z + dz) % 4 * 4 + (x + dx) % 4
    entry = lax.broadcasted_iota(jnp.int32, (128, 256), 0)
    slot32 = lax.broadcasted_iota(jnp.int32, (32, 256), 1)
    row32 = lax.broadcasted_iota(jnp.int32, (32, 256), 0)
    for h in range(2):
        infos = s.info[2 * h : 2 * h + 2].reshape(32, 128).astype(bf16)
        picked = [
            jnp.dot(
                infos,
                jnp.where(entry == taker + EXPERTS * i, 1.0, 0.0).astype(bf16),
                preferred_element_type=f32,
            )
            for i in range(4)
        ]
        hit = (picked[0] == (slot32 % CAP).astype(f32)) & (slot32 // CAP % 2 == row32 // ROWS)
        s.placing[h] = jnp.where(hit, 1.0, 0.0).astype(bf16)
        for i in range(3):
            s.weighting[h, 32 * i : 32 * i + 32, :] = jnp.where(hit, picked[i + 1], 0.0).astype(bf16)

    def sums_copy(h, t):
        return remote(
            s.sums.at[h, t],
            s.sums_in.at[h, t],
            s.sums_send.at[h, t],
            s.sums_recv.at[h, t],
            (replica, group_shifted(expert, t, -1)),
        )

    loads[0].wait()
    to_core[0].wait_recv()
    for copy in to_core[4:]:
        copy.wait_recv()
    to_core[3].start()
    for h in (1, 0):

        @pl.loop(1 - h, 8)
        def _(t):
            heads_copy(h, t).wait_recv()

        for q in range(2):

            @pl.loop(0, quarter // TILE)
            def _(n):
                value = jnp.dot(
                    s.heads[h].reshape(8 * ROWS, quarter),
                    s.v_proj[q, :, columns(n)],
                    preferred_element_type=f32,
                )
                at = pl.multiple_of(q * quarter + n * TILE, TILE)
                s.sums[h, :, :, pl.ds(at, TILE)] = value.astype(bf16).reshape(8, ROWS, TILE)

        @pl.loop(1, 8)
        def _(t):
            sums_copy(h, t).start()

    over = [
        remote(
            s.rows_all.at[h, pl.ds(0, ROWS)],
            s.rows_all.at[h, pl.ds(ROWS, ROWS)],
            s.over_send.at[h],
            s.over_recv.at[h],
            across,
        )
        for h in range(2)
    ]

    def finish_rows(h):
        @pl.loop(1, 8)
        def _(t):
            sums_copy(h, t).wait_recv()

        rows = pl.ds(ROWS * h, ROWS)

        @pl.loop(0, half // TILE)
        def _(n):
            total = s.mid[rows, columns(n)] + s.sums[h, 0, :, columns(n)].astype(f32)
            for t in range(1, 8):
                total = total + s.sums_in[h, t, :, columns(n)].astype(f32)
            s.mid[rows, columns(n)] = total
            s.rows_all[h, :ROWS, columns(n)] = (total * s.gain[:, columns(n)]).astype(bf16)

        over[h].start()
        mid = s.mid[rows, :]
        s.square_out[rows, :] = jnp.broadcast_to(
            jnp.sum(mid * mid, axis=-1, keepdims=True), (ROWS, 128)
        )

    def dispatch(h, i):
        rows = pl.ds(pl.multiple_of(i * 16, 16), 16)
        return remote(
            s.outgoing.at[h, rows],
            s.block.at[h, rows],
            s.disp_send.at[h, i],
            s.disp_recv.at[h, i],
            (replica, shifted(expert, i, 1)),
        )

    def send_rows(h, c):
        if c == 0:
            over[h].wait_recv()
        first, number = CHUNKS[c]
        slots = pl.ds(16 * first, 16 * number)

        @pl.loop(0, half // TILE)
        def _(n):
            s.outgoing[h, slots, columns(n)] = lax.dot_general(
                s.placing[h, :, slots],
                s.rows_all[h, :, columns(n)],
                (((0,), (0,)), ((), ())),
                preferred_element_type=f32,
            ).astype(bf16)

        @pl.loop(max(1, first), first + number)
        def _(i):
            dispatch(h, i).start()

        if first == 0:
            s.block[h, :16, :] = s.outgoing[h, :16, :]

    finish_rows(1)
    send_rows(1, 0)
    finish_rows(0)
    squares = [
        remote(
            s.square_out, s.square_in.at[i], s.square_send.at[i], s.square_recv.at[i], device
        )
        for i, device in enumerate((beside, across, diagonal))
    ]
    for copy in squares:
        copy.start()
    send_rows(1, 1)
    send_rows(0, 0)

    def scale_copy(i):
        slots = pl.ds(pl.multiple_of(i * 16, 16), 16)
        return remote(
            s.scale_out.at[slots],
            s.scale_in.at[slots],
            s.scale_send.at[i],
            s.scale_recv.at[i],
            (replica, shifted(expert, i, 1)),
        )

    def send_scales():
        for copy in squares:
            copy.wait_recv()
        total = jnp.concatenate(
            [
                s.square_out[:ROWS, :] + s.square_in[0, ROWS:, :],
                s.square_in[1, :ROWS, :] + s.square_in[2, ROWS:, :],
            ],
            axis=0,
        )
        rest = lax.rsqrt(total / (2.0 * half) + 1e-06)
        value = jnp.zeros((256, 128), f32)
        for _ in range(3):
            piece = rest.astype(bf16)
            value = value + lax.dot_general(
                s.placing[0], piece, (((0,), (0,)), ((), ())), preferred_element_type=f32
            )
            rest = rest - piece.astype(f32)
        s.scale_out[...] = value

        @pl.loop(1, 16)
        def _(i):
            scale_copy(i).start()

        s.scale_in[:16, :] = value[:16]

    tiles = hidden // TILE

    def slots_of(c, chunks=CHUNKS):
        first, number = chunks[c]
        return pl.ds(16 * first, 16 * number)

    def gate_up(h, c, n):
        for which, mats in enumerate((s.v_gate, s.v_up)):
            yield which, jnp.dot(
                s.block[h, slots_of(c), :quarter],
                mats[0, :, columns(n)],
                preferred_element_type=f32,
            ) + jnp.dot(
                s.block[h, slots_of(c), quarter:],
                mats[1, :, columns(n)],
                preferred_element_type=f32,
            )

    def part_copy(c, n):
        return remote(
            s.part_out.at[n, :, slots_of(c)],
            s.part_in.at[n, :, slots_of(c)],
            s.part_send.at[c, n],
            s.part_recv.at[c, n],
            beside,
        )

    def wait_rows(h, c):
        first, number = CHUNKS[c]

        @pl.loop(max(1, first), first + number)
        def _(i):
            dispatch(h, i).wait_recv()

    loads[1].wait()
    loads[2].wait()
    to_core[1].wait_recv()
    to_core[2].wait_recv()
    for c in range(len(CHUNKS)):
        wait_rows(1, c)

        @pl.loop(0, tiles)
        def _(n):
            for which, value in gate_up(1, c, n):
                s.part_out[n, which, slots_of(c), :] = value.astype(bf16)
            part_copy(c, n).start()

        if c == 0:
            send_rows(0, 1)
            send_scales()

    def own_part(c):
        wait_rows(0, c)

        @pl.loop(0, tiles)
        def _(n):
            for which, value in gate_up(0, c, n):
                s.part_own[n, which, slots_of(c), :] = value

    def give_back(h, i):
        rows = pl.ds(pl.multiple_of(i * 16, 16), 16)
        return remote(
            s.result.at[h, rows],
            s.returned.at[h, rows],
            s.ret_send.at[h, i],
            s.ret_recv.at[h, i],
            (replica, shifted(expert, i, -1)),
        )

    def down(h, c, chunks):
        first, number = chunks[c]
        for q in range(2):

            @pl.loop(0, quarter // TILE)
            def _(n):
                value = jnp.zeros((16 * number, TILE), f32)
                for k in range(tiles):
                    value = value + jnp.dot(
                        s.units[h, k, slots_of(c, chunks), :],
                        s.v_down[q, k * TILE : (k + 1) * TILE, columns(n)],
                        preferred_element_type=f32,
                    )
                at = pl.multiple_of(q * quarter + n * TILE, TILE)
                s.result[h, slots_of(c, chunks), pl.ds(at, TILE)] = value.astype(bf16)

        @pl.loop(max(1, first), first + number)
        def _(i):
            give_back(h, i).start()

        if first == 0:
            s.returned[h, :16, :] = s.result[h, :16, :]

    def unit_copy(c, n):
        return remote(
            s.units.at[0, n, slots_of(c, SHARES)],
            s.units.at[1, n, slots_of(c, SHARES)],
            s.unit_send.at[c, n],
            s.unit_recv.at[c, n],
            beside,
        )

    def combine(h, begin, end):
        @pl.loop(max(1, begin), end)
        def _(i):
            give_back(h, i).wait_recv()

        slots = pl.ds(16 * begin, 16 * (end - begin))

        @pl.loop(0, half // TILE)
        def _(n):
            three = jnp.dot(
                s.weighting[h, :, slots],
                s.returned[h, slots, columns(n)],
                preferred_element_type=f32,
            )
            value = three[:32] + three[32:64] + three[64:]
            s.mixed[h, :, columns(n)] = value if begin == 0 else s.mixed[h, :, columns(n)] + value

    @pl.loop(1, 16)
    def _(i):
        scale_copy(i).wait_recv()

    own_part(0)
    for c in range(len(CHUNKS)):

        @pl.loop(0, tiles)
        def _(n):
            part_copy(c, n).wait_recv()
            scale = s.scale_in[slots_of(c), :1]
            gate = s.part_own[n, 0, slots_of(c), :] + s.part_in[n, 0, slots_of(c), :].astype(f32)
            up_val = s.part_own[n, 1, slots_of(c), :] + s.part_in[n, 1, slots_of(c), :].astype(f32)
            gate, up_val = gate * scale, up_val * scale
            s.units[0, n, slots_of(c), :] = (gate / (1.0 + jnp.exp(-gate)) * up_val).astype(bf16)
            unit_copy(c, n).start()

        if c == 1:

            @pl.loop(0, tiles)
            def _(n):
                unit_copy(2, n).start()

        if c == 0:
            loads[3].wait()
            to_core[3].wait_recv()
        if c + 1 < len(CHUNKS):
            own_part(c + 1)
        down(0, c, CHUNKS)
    last = [
        remote(s.last_out.at[i], s.last_in.at[i], s.last_send.at[i], s.last_recv.at[i], device)
        for i, device in enumerate((across, beside, diagonal))
    ]
    for c in range(len(SHARES)):

        @pl.loop(0, tiles)
        def _(n):
            unit_copy(c, n).wait_recv()

        down(1, c, SHARES)
    combine(0, 0, 16)
    s.last_out[0] = s.mixed[0, 16:, :].astype(bf16)
    last[0].start()
    for copy in along + early + to_core + onward + over + squares:
        copy.wait_send()

    @pl.loop(1, 8)
    def _(i):
        heads_copy(0, i).wait_send()
        heads_copy(1, i).wait_send()
        sums_copy(0, i).wait_send()
        sums_copy(1, i).wait_send()
        give_back(1, i).wait_send()

    heads_copy(1, 0).wait_send()

    @pl.loop(1, 16)
    def _(i):
        dispatch(0, i).wait_send()
        dispatch(1, i).wait_send()
        scale_copy(i).wait_send()
        give_back(0, i).wait_send()

    @pl.loop(0, tiles)
    def _(n):
        part_copy(0, n).wait_send()
        part_copy(1, n).wait_send()
        unit_copy(0, n).wait_send()

    combine(1, 0, 8)
    combine(1, 8, 12)
    combine(1, 12, 16)
    s.last_out[1] = (s.mid[16:, :] + s.mixed[1, :16, :]).astype(bf16)
    s.last_out[2] = s.mixed[1, 16:, :].astype(bf16)
    last[1].start()
    last[2].start()
    for copy in last:
        copy.wait_recv()
    here = s.mid[:16, :] + s.mixed[0, :16, :]
    refs.near_sum[:, quarter_of(replica)] = here[:, :quarter]
    refs.near_sum[:, quarter_of(sibling)] = here[:, quarter:]
    there = s.last_in[1].astype(f32)
    refs.near_sum[:, quarter_of(other_replica)] = there[:, :quarter]
    refs.near_sum[:, quarter_of(other_sibling)] = there[:, quarter:]
    refs.far_sum[:, quarter_of(replica)] = s.last_in[0, :, :quarter]
    refs.far_sum[:, quarter_of(sibling)] = s.last_in[0, :, quarter:]
    refs.far_sum[:, quarter_of(other_replica)] = s.last_in[2, :, :quarter]
    refs.far_sum[:, quarter_of(other_sibling)] = s.last_in[2, :, quarter:]

    for copy in last:
        copy.wait_send()

    @pl.loop(8, 16)
    def _(i):
        give_back(1, i).wait_send()

    @pl.loop(0, tiles)
    def _(n):
        unit_copy(1, n).wait_send()
        unit_copy(2, n).wait_send()


ARGS = (
    "hidden_in",
    "query",
    "key_new",
    "value_new",
    "key_cache",
    "value_cache",
    "cache_len",
    "attn_out_w",
    "norm_gain",
    "routes",
    "gate_weights",
    "w_gate",
    "w_up",
    "w_down",
)


SMALL = (
    "query",
    "key_new",
    "value_new",
    "routes",
    "gate_weights",
    "hidden_in",
    "norm_gain",
)


def body(*args):
    f32, bf16 = jnp.float32, jnp.bfloat16
    given = dict(zip(ARGS, args))
    given["norm_gain"] = given["norm_gain"][None, :]
    given["routes"], given["gate_weights"] = given["routes"].T, given["gate_weights"].T
    n_rows, width = given["hidden_in"].shape
    groups, context, head_size = given["key_cache"].shape[1:]
    heads = given["query"].shape[1] // head_size
    _, quarter, hidden = given["w_gate"].shape
    deep = given["attn_out_w"].shape[0]
    half, tiles = 2 * quarter, hidden // TILE
    vmem, anywhere = pl.BlockSpec(memory_space=pltpu.VMEM), pl.BlockSpec(memory_space=pl.ANY)
    places = {name: anywhere for name in ARGS}
    places["cache_len"] = pl.BlockSpec(memory_space=pltpu.SMEM)
    scratch = {"in_" + name: (given[name].shape, given[name].dtype) for name in SMALL}
    scratch |= dict(
        k_ring=((RING, groups, context, head_size), bf16),
        v_ring=((RING, groups, context, head_size), bf16),
        q_rows=((n_rows, heads, head_size), f32),
        o_rows=((n_rows, heads, head_size), f32),
        scores=((RING, heads, context), f32),
        probs=((RING, heads, context), bf16),
        own_part=((RING, heads, head_size), f32),
        k_new=((n_rows, groups, head_size), f32),
        v_new=((n_rows, groups, head_size), f32),
        info=((4, ROWS, 128), f32),
        hid_out=((ROWS, half), bf16),
        hid_in=((ROWS, half), bf16),
        mid=((32, half), f32),
        gain=((1, half), f32),
        v_proj=((2, 4 * deep, quarter), bf16),
        v_gate=((2, quarter, hidden), bf16),
        v_up=((2, quarter, hidden), bf16),
        v_down=((2, hidden, quarter), bf16),
        attn=((8, ROWS, quarter), bf16),
        heads=((2, 8, ROWS, quarter), bf16),
        sums=((2, 8, ROWS, half), bf16),
        sums_in=((2, 8, ROWS, half), bf16),
        placing=((2, 32, 256), bf16),
        weighting=((2, 96, 256), bf16),
        square_out=((32, 128), f32),
        square_in=((3, 32, 128), f32),
        scale_out=((256, 128), f32),
        scale_in=((256, 128), f32),
        rows_all=((2, 32, half), bf16),
        outgoing=((2, 256, half), bf16),
        block=((2, 256, half), bf16),
        part_out=((tiles, 2, 256, TILE), bf16),
        part_in=((tiles, 2, 256, TILE), bf16),
        part_own=((tiles, 2, 256, TILE), f32),
        units=((2, tiles, 256, TILE), bf16),
        result=((2, 256, half), bf16),
        returned=((2, 256, half), bf16),
        mixed=((2, 32, half), f32),
        last_out=((3, 16, half), bf16),
        last_in=((3, 16, half), bf16),
    )
    semaphores = dict(
        k_sem=(RING,),
        v_sem=(RING,),
        load_sem=(4,),
        small_sem=(len(SMALL),),
        x_send=(6,),
        x_recv=(6,),
        core_send=(7,),
        core_recv=(7,),
        early_send=(4,),
        early_recv=(4,),
        heads_send=(2, 8),
        heads_recv=(2, 8),
        sums_send=(2, 8),
        sums_recv=(2, 8),
        over_send=(2,),
        over_recv=(2,),
        square_send=(3,),
        square_recv=(3,),
        scale_send=(16,),
        scale_recv=(16,),
        disp_send=(2, 16),
        disp_recv=(2, 16),
        part_send=(len(CHUNKS), tiles),
        part_recv=(len(CHUNKS), tiles),
        unit_send=(len(SHARES), tiles),
        unit_recv=(len(SHARES), tiles),
        ret_send=(2, 16),
        ret_recv=(2, 16),
        last_send=(3,),
        last_recv=(3,),
    )
    names = ARGS + ("near_sum", "far_sum")
    scratch_names = list(scratch) + list(semaphores)

    def kernel(*all_refs):
        layer_kernel(names, scratch_names, *all_refs)

    near_sum, far_sum = pl.pallas_call(
        kernel,
        out_shape=(
            jax.ShapeDtypeStruct((n_rows, width), f32),
            jax.ShapeDtypeStruct((n_rows, width), bf16),
        ),
        in_specs=[places[name] for name in ARGS],
        out_specs=(vmem, vmem),
        scratch_shapes=[pltpu.VMEM(*v) for v in scratch.values()]
        + [pltpu.SemaphoreType.DMA(v) for v in semaphores.values()],
        compiler_params=pltpu.CompilerParams(
            collective_id=0, has_side_effects=True, vmem_limit_bytes=60 * 1024 * 1024
        ),
        cost_estimate=pl.CostEstimate(
            flops=12 * 10**9, bytes_accessed=40 * 10**6, transcendentals=10**6
        ),
    )(*given.values())
    return (near_sum + far_sum.astype(f32)).astype(bf16)


def solution(mesh):
    placed = (
        P(("replica", "expert"), None),
        P(("replica", "expert"), None),
        P(("replica", "expert"), None),
        P(("replica", "expert"), None),
        P(("replica", "expert"), None, None, None),
        P(("replica", "expert"), None, None, None),
        P(("replica", "expert")),
        P("expert", "replica"),
        P(),
        P(("replica", "expert"), None),
        P(("replica", "expert"), None),
        P("expert", "replica", None),
        P("expert", "replica", None),
        P("expert", None, "replica"),
    )
    return jax.shard_map(
        body, mesh=mesh, in_specs=placed, out_specs=P(("replica", "expert"), None), check_vma=False
    )
```
